128 devices in a mesh: rows: 16 (over y_hi, x, core), inner: 8 (over z, y_lo).
Axes of the slice: x: 4, y: 4 (y_hi: 2, y_lo: 2; y = y_hi * 2 + y_lo), z: 4, core: 2. Of those that a mesh axis runs over, the one named last changes fastest.
Arguments:
- h_blocks: bfloat16 [64, 8, 128, 128], P('rows'), may hold values from -6 to 6
- h_cols: int32 [64, 8], P('rows'), may hold values from 0 to 63, as said below
- h_count: int32 [64], P('rows'), may hold values from 1 to 8, as said below
- z_blocks: bfloat16 [64, 8, 128, 128], P('rows'), may hold values from -0.1875 to 0.1875
- z_cols: int32 [64, 8], P('rows'), may hold values from 0 to 63, as said below
- z_count: int32 [64], P('rows'), may hold values from 1 to 8, as said below
- x_perp: bfloat16 [8192, 8192], P('rows', 'inner'), may hold values from -6 to 6
Outputs:
- h_perp: bfloat16 [8192, 8192], P('rows', 'inner')
- x_out: bfloat16 [8192, 8192], P('rows', 'inner')
The draws below stay inside these ranges and needn't reach their ends.
Inputs may be any that keep to these rules, and one draw needn't show every extreme that they name: `h_cols`: slot s of every block row, live or padded, names a block column of stripe s, that is from (s) * 8 to (s + 1) * 8 - 1; a row may name a column twice. `z_cols`: slot s of every block row, live or padded, names a block column of stripe s, that is from (s) * 8 to (s + 1) * 8 - 1; a row may name a column twice. The live slots of block row i are slots 0 to h_count[i] - 1. The live slots of block row k are slots 0 to z_count[k] - 1.
All inputs are finite; a program needn't handle non-finite values.
Results may differ from the reference program's by a relative error of at most 0.0049.
Values may be sent and summed in bfloat16 or wider, within the bound.
No kernel may reach another device: no remote copies, remote signals or barrier semaphores. Data moves between devices by JAX's collectives and lax.ppermute only.
A program may use at most 192 MiB of HBM per device.

```python
import jax
import jax.numpy as jnp
from jax import lax

BLOCK = 128
SLOTS = 8
NB = 64
ORBITALS = 8192
STRIPE = 8
SLOT_GROUP = 1


def stripe_columns(key):
    drawn_cols = jax.random.randint(key, (NB, SLOTS), 0, STRIPE).astype(jnp.int32)
    offsets = (jnp.arange(SLOTS) // SLOT_GROUP * STRIPE).astype(jnp.int32)
    columns = drawn_cols + offsets[None, :]
    places = jax.random.randint(jax.random.fold_in(key, 5), (2,), 0, NB).astype(jnp.int32)
    columns = columns.at[places[0], SLOTS - 1].set(NB - 1)
    return columns.at[places[1], 0].set(0)


def live_counts(key):
    values = jax.random.randint(key, (NB,), 1, SLOTS + 1).astype(jnp.int32)
    places = jax.random.randint(jax.random.fold_in(key, 5), (2,), 0, NB).astype(jnp.int32)
    values = values.at[places[0]].set(1)
    return values.at[places[1]].set(SLOTS)


def draw_h_cols(key, part):
    key = jax.random.fold_in(key, 11)
    return stripe_columns(key)


def draw_z_cols(key, part):
    key = jax.random.fold_in(key, 12)
    return stripe_columns(key)


def draw_h_count(key, part):
    key = jax.random.fold_in(key, 13)
    return live_counts(key)


def draw_z_count(key, part):
    key = jax.random.fold_in(key, 14)
    return live_counts(key)


def level_of(own_key, extent, cuts, least, top_value):
    def one(position, shards_of):
        heights = jax.random.uniform(jax.random.fold_in(jax.random.fold_in(own_key, 6), position), (shards_of,), jnp.float32, least / len(cuts), top_value / len(cuts))
        return jnp.repeat(jnp.exp(heights), extent[position] // shards_of).reshape((-1,) + (1,) * (len(extent) - position - 1))

    loudness = one(*cuts[0])
    for cut in cuts[1:]:
        loudness = loudness * one(*cut)
    return loudness


def centred(own_key, shape, scale, bound, split=(), held_as=jnp.bfloat16):
    result = jax.random.normal(own_key, shape, jnp.float32) * scale
    if len(split) > 0:
        result = level_of(own_key, shape, split, -0.22, 0.18) * result
    return jnp.clip(result, min=-bound, max=bound).astype(held_as)


def setup_inputs(seed: int = 0) -> dict:
    splits = jax.random.split(jax.random.key(seed), 8)
    h_blocks = centred(splits[0], (NB, SLOTS, BLOCK, BLOCK), 1.0, 6.0, ((0, 16),))
    h_cols = draw_h_cols(jax.random.fold_in(splits[7], 71), 0)
    h_count = draw_h_count(jax.random.fold_in(splits[7], 71), 0)
    z_blocks = centred(splits[3], (NB, SLOTS, BLOCK, BLOCK), (SLOTS * BLOCK) ** -0.5, 0.1875, ((0, 16),))
    z_cols = draw_z_cols(jax.random.fold_in(splits[7], 71), 0)
    z_count = draw_z_count(jax.random.fold_in(splits[7], 71), 0)
    x_perp = centred(splits[6], (ORBITALS, ORBITALS), 1.0, 6.0, ((0, 16), (1, 8)))
    return {"h_blocks": h_blocks, "h_cols": h_cols, "h_count": h_count, "z_blocks": z_blocks, "z_cols": z_cols, "z_count": z_count, "x_perp": x_perp}


def masked(blocks, counts):
    live = jnp.arange(SLOTS)[None, :] < counts[:, None]
    return jnp.where(live[:, :, None, None], blocks, jnp.zeros((), blocks.dtype))


def reference(h_blocks, h_cols, h_count, z_blocks, z_cols, z_count, x_perp):
    h_live = masked(h_blocks, h_count)
    z_live = masked(z_blocks, z_count)
    full_width = NB * BLOCK
    block_ids = jnp.arange(NB).astype(jnp.int32)

    def product_row(inputs):
        h_row, h_names = inputs
        z_rows = z_live[h_names].astype(jnp.float32)
        z_names = z_cols[h_names].astype(jnp.int32)
        pieces = jnp.einsum('spq,stqr->stpr', h_row.astype(jnp.float32), z_rows)
        placing = (z_names[:, :, None] == block_ids[None, None, :]).astype(jnp.float32)
        row_sum = jnp.einsum('stj,stpr->pjr', placing, pieces)
        return row_sum.reshape(BLOCK, full_width).astype(jnp.bfloat16)

    product = lax.map(product_row, (h_live, h_cols))

    def add_row(running, inputs):
        z_row, z_names, m_row = inputs
        pieces = jnp.einsum('tpq,pj->tqj', z_row.astype(jnp.float32), m_row.astype(jnp.float32))
        return running.at[z_names].add(pieces), None

    h_total, unused = lax.scan(add_row, jnp.zeros((NB, BLOCK, full_width), jnp.float32), (z_live, z_cols, product))
    h_perp = h_total.reshape(full_width, full_width).astype(jnp.bfloat16)

    x_three = x_perp.reshape(full_width, NB, BLOCK)

    def coupled_row(inputs):
        z_row, z_names = inputs
        columns = x_three[:, z_names, :].astype(jnp.float32)
        return jnp.einsum('tqp,atp->qa', z_row.astype(jnp.float32), columns).astype(jnp.bfloat16)

    coupled_t = lax.map(coupled_row, (z_live, z_cols))
    coupled_flat = coupled_t.reshape(full_width, NB, BLOCK)

    def output_row(inputs):
        z_row, z_names = inputs
        picked = coupled_flat[:, z_names, :].astype(jnp.float32)
        return jnp.einsum('tqp,ktp->qk', z_row.astype(jnp.float32), picked).astype(jnp.bfloat16)

    x_out = lax.map(output_row, (z_live, z_cols)).reshape(full_width, full_width)
    return h_perp, x_out
```

```python
import functools

import jax
import jax.numpy as jnp
from jax import lax
from jax.experimental import pallas as pl
from jax.experimental.pallas import tpu as pltpu
from jax.sharding import PartitionSpec as P

AXES = ("rows", "inner")
B = 128
BF = jnp.bfloat16
F32 = jnp.float32
VMEM_LIMIT = 48 * 1024 * 1024
ZC, HC, ZN, HN = 0, 8, 16, 17
PX, PYH, PP, PZ, PYL, PM, PC, PR = range(8)


def places():
    for yh in range(2):
        for x in range(4):
            for p in range(2):
                for z in range(4):
                    for yl in range(2):
                        yield yh, x, p, z, yl


def number(yh, x, p, z, yl):
    return (((yh * 4 + x % 4) * 2 + p) * 4 + z % 4) * 2 + yl


def send(value, to):
    return lax.ppermute(value, AXES, [(number(*at), number(*to(*at))) for at in places()])


def along_x(d):
    return lambda yh, x, p, z, yl: (yh, (x + d) % 4, p, z, yl)


def along_z(d):
    return lambda yh, x, p, z, yl: (yh, x, p, (z + d) % 4, yl)


def other_yh(yh, x, p, z, yl):
    return 1 - yh, x, p, z, yl


def other_yl(yh, x, p, z, yl):
    return yh, x, p, z, 1 - yl


def other_core(yh, x, p, z, yl):
    return yh, x, 1 - p, z, yl


def to_chip(dy, dx):
    return lambda yh, x, p, z, yl: ((yh + dy) % 2, (x + dx) % 4, p, z, yl)


def transposed(yh, x, p, z, yl):
    m, c = yh * 4 + x, z * 2 + yl
    return c // 4, c % 4, p, m // 2, m % 2


def pieces_of(rows):
    half = rows // 2
    out = []
    for pair in (0, 1):
        out += [(0, pair, 0, rows), (-1, pair, 0, rows), (1, pair, 0, rows), (2, pair, 0, half), (2, pair, half, half)]
    return out


def gather_chips(v, ring, pair):
    half = v.shape[0] // 2
    y = send(v, pair)
    out = []
    for w in (v, y):
        a = send(w, ring(1))
        b = send(w, ring(-1))
        a2 = send(a[:half], ring(1))
        b2 = send(b[half:], ring(-1))
        out += [w, a, b, a2, b2]
    return out


def vmem_call(kernel, scalars, arrays, out_shape, scratch, flops):
    whole = pl.BlockSpec(memory_space=pltpu.VMEM)
    many = isinstance(out_shape, (list, tuple))
    outs = list(out_shape) if many else [out_shape]
    size = sum(a.size * a.dtype.itemsize for a in list(arrays) + outs)
    return pl.pallas_call(
        kernel,
        out_shape=out_shape,
        grid_spec=pltpu.PrefetchScalarGridSpec(
            num_scalar_prefetch=len(scalars),
            grid=(),
            in_specs=[whole] * len(arrays),
            out_specs=[whole] * len(outs) if many else whole,
            scratch_shapes=scratch,
        ),
        compiler_params=pltpu.CompilerParams(vmem_limit_bytes=VMEM_LIMIT),
        cost_estimate=pl.CostEstimate(flops=flops, bytes_accessed=size, transcendentals=0),
    )(*scalars, *arrays)


def inner_stripe(pos, dz, dyl):
    return lax.rem(pos[PZ] + dz + 4, 4) * 2 + lax.rem(pos[PYL] + dyl, 2)


def chip_of(pos, dx, dyh):
    return lax.rem(pos[PYH] + dyh, 2) * 4 + lax.rem(pos[PX] + dx + 4, 4)


def coupled_kernel(pieces, table, pos, *refs):
    n = len(pieces)
    xs, (z_own, z_sib, out, lhs, rhs) = refs[:n], refs[n:]
    c, p = pos[PC], pos[PP]

    def one(source, core, j):
        row = c * 8 + core * 4 + j
        live = table[row, ZN]
        for ref, (dz, dyl, lo, size) in zip(xs, pieces):
            t = inner_stripe(pos, dz, dyl)
            col = table[row, ZC + t] - t * 8
            spot = (dz % 4) * 2 + dyl
            lhs[lo : lo + size, spot * B : spot * B + B] = ref[:, pl.ds(pl.multiple_of(col * B, B), B)]
            if lo == 0:
                block = source[j, t]
                rhs[:, spot * B : spot * B + B] = jnp.where(t < live, block, jnp.zeros_like(block))
        total = lax.dot_general(lhs[...], rhs[...], (((1,), (1,)), ((), ())), preferred_element_type=F32)
        out[:, pl.ds(pl.multiple_of((core * 4 + j) * B, B), B)] = total.astype(BF)

    @pl.loop(0, 4)
    def _(j):
        one(z_own, p, j)
        one(z_sib, 1 - p, j)


def x_out_kernel(pieces, table, pos, *refs):
    n = len(pieces)
    blocks, (z_own, z_sib, mine, theirs) = refs[:n], refs[n:]
    p, r = pos[PP], pos[PR]
    for source, acc, core_row in ((z_own, mine, r), (z_sib, theirs, r + 1 - 2 * p)):
        acc[...] = jnp.zeros_like(acc)

        @pl.loop(0, 4)
        def _(i):
            row = core_row * 4 + i
            live = table[row, ZN]
            here = pl.ds(pl.multiple_of(i * B, B), B)
            for ref, (dx, dyh, lo, size) in zip(blocks, pieces):
                t = chip_of(pos, dx, dyh)
                q = table[row, ZC + t] - t * 8 - p * 4 - lo // B

                @pl.when((t < live) & (q >= 0) & (q < size // B))
                def _():
                    rows = pl.ds(pl.multiple_of(q * B, B), B)
                    acc[here, :] += jnp.dot(source[i, t], ref[rows, :], preferred_element_type=F32)


def w_kernel(table, pos, z_own, z_sib, shared, out, acc):
    p, m, c = pos[PP], pos[PM], pos[PC]
    acc[...] = jnp.zeros_like(acc)
    for source, core in ((z_own, p), (z_sib, 1 - p)):
        for d in range(8):
            chip = chip_of(pos, -(d % 4), d // 4)

            @pl.loop(0, 4)
            def _(j):
                k = chip * 8 + core * 4 + j
                i = table[k, ZC + m] - m * 8 - p * 4
                col = table[k, HC + c] - c * 8

                @pl.when((m < table[k, ZN]) & (c < table[k, HN]) & (i >= 0) & (i < 4))
                def _():
                    term = lax.dot_general(
                        source[d, j],
                        shared[chip * 2 + core, 4 + j],
                        (((0,), (0,)), ((), ())),
                        preferred_element_type=F32,
                    )
                    acc[pl.ds(pl.multiple_of(i * B, B), B), pl.ds(pl.multiple_of(col * B, B), B)] += term

    out[...] = acc[...].astype(BF)


def h_perp_kernel(pieces, table, pos, *refs):
    n = len(pieces)
    blocks, (shared, out, acc) = refs[:n], refs[n:]
    c = pos[PC]
    acc[...] = jnp.zeros_like(acc)

    @pl.loop(0, 8)
    def _(j):
        for ref, (dz, dyl, lo, size) in zip(blocks, pieces):
            t = inner_stripe(pos, dz, dyl)
            row = t * 8 + j
            col = table[row, ZC + c] - c * 8

            @pl.when(c < table[row, ZN])
            def _():
                term = jnp.dot(
                    ref[:, pl.ds(pl.multiple_of(j * B, B), B)],
                    shared[row // 4, lax.rem(row, 4)],
                    preferred_element_type=F32,
                )
                acc[lo : lo + size, pl.ds(pl.multiple_of(col * B, B), B)] += term

    out[...] = acc[...].astype(BF)


def body(h_blocks, h_cols, h_count, z_blocks, z_cols, z_count, x_perp):
    r, c = lax.axis_index("rows"), lax.axis_index("inner")
    m, p = r // 2, r % 2
    yh, x, z, yl = m // 4, m % 4, c // 2, c % 2
    pos = jnp.stack([x, yh, p, z, yl, m, c, r]).astype(jnp.int32)

    mine = jnp.concatenate([z_cols, h_cols, z_count[:, None], h_count[:, None]], axis=1)
    table = lax.dynamic_update_slice(jnp.zeros((64, 18), jnp.int32), mine, (r * 4, 0))
    table = table + send(table, other_core)
    table = table + send(table, other_yh)
    table = table + (send(table, along_x(1)) + send(table, along_x(-1)) + send(table, along_x(2)))

    x_pieces = gather_chips(x_perp, along_z, other_yl)
    z_stripe = send(z_blocks, transposed)
    z_stripe_sib = send(z_stripe, other_core)
    z_sib = send(z_blocks, other_core)

    slot_c = jnp.concatenate(
        [lax.dynamic_index_in_dim(v, c, 1, keepdims=False) for v in (z_blocks, h_blocks)], axis=0
    )
    shared = lax.all_gather(slot_c[None], "rows", axis=0, tiled=True)
    named = []
    for d in range(8):
        dy, dx = d // 4, d % 4
        slot = (yh + dy) % 2 * 4 + (x + dx) % 4
        block = lax.dynamic_index_in_dim(z_blocks, slot, 1, keepdims=False)
        named.append(send(block, to_chip(dy, dx)) if d else block)
    named = jnp.stack(named)
    named_sib = send(named, other_core)

    tile = jax.ShapeDtypeStruct((512, 1024), BF)
    wide = jax.ShapeDtypeStruct((512, 1024), F32)
    pieces = pieces_of(512)
    dense = 2 * 64 * 512 * B * B
    w_tile = vmem_call(
        w_kernel, (table, pos), (named, named_sib, shared), tile, [pltpu.VMEM((512, 1024), F32)], dense // 4
    )
    coupled = vmem_call(
        functools.partial(coupled_kernel, pieces),
        (table, pos),
        (*x_pieces, z_stripe, z_stripe_sib),
        tile,
        [pltpu.VMEM((512, 1024), BF), pltpu.VMEM((B, 1024), BF)],
        dense,
    )
    c_pieces = gather_chips(coupled, along_x, other_yh)
    w_pieces = gather_chips(w_tile, along_z, other_yl)
    x_mine, x_theirs = vmem_call(
        functools.partial(x_out_kernel, pieces), (table, pos), (*c_pieces, z_blocks, z_sib), [wide, wide], [], dense
    )
    x_tile = (x_mine + send(x_theirs, other_core)).astype(BF)
    h_tile = vmem_call(
        functools.partial(h_perp_kernel, pieces),
        (table, pos),
        (*w_pieces, shared),
        tile,
        [pltpu.VMEM((512, 1024), F32)],
        dense,
    )
    return h_tile, x_tile


def solution(mesh):
    in_specs = (
        P("rows", None, None, None),
        P("rows", None),
        P("rows"),
        P("rows", None, None, None),
        P("rows", None),
        P("rows"),
        P("rows", "inner"),
    )
    out_specs = (P("rows", "inner"), P("rows", "inner"))
    return jax.shard_map(body, mesh=mesh, in_specs=in_specs, out_specs=out_specs, check_vma=False)
```

```python
import functools

import jax
import jax.numpy as jnp
from jax import lax
from jax.experimental import pallas as pl
from jax.experimental.pallas import tpu as pltpu
from jax.sharding import PartitionSpec as P

AXES = ("rows", "inner")
B = 128
BF = jnp.bfloat16
F32 = jnp.float32
VMEM_LIMIT = 48 * 1024 * 1024
ZC, HC, ZN, HN = 0, 8, 16, 17
PX, PYH, PP, PZ, PYL, PM, PC, PR = range(8)


def places():
    for yh in range(2):
        for x in range(4):
            for p in range(2):
                for z in range(4):
                    for yl in range(2):
                        yield yh, x, p, z, yl


def number(yh, x, p, z, yl):
    return (((yh * 4 + x % 4) * 2 + p) * 4 + z % 4) * 2 + yl


def send(value, to):
    return lax.ppermute(value, AXES, [(number(*at), number(*to(*at))) for at in places()])


def along_x(d):
    return lambda yh, x, p, z, yl: (yh, (x + d) % 4, p, z, yl)


def along_z(d):
    return lambda yh, x, p, z, yl: (yh, x, p, (z + d) % 4, yl)


def other_yh(yh, x, p, z, yl):
    return 1 - yh, x, p, z, yl


def other_yl(yh, x, p, z, yl):
    return yh, x, p, z, 1 - yl


def other_core(yh, x, p, z, yl):
    return yh, x, 1 - p, z, yl


OWN, UP, DOWN, FAR = (0, 0), (-1, 0), (1, 0), (2, 0)
PAIR, PAIR_UP, PAIR_DOWN, PAIR_FAR = (0, 1), (-1, 1), (1, 1), (2, 1)
GATHERED = (OWN, DOWN, FAR, UP, PAIR, PAIR_DOWN, PAIR_FAR, PAIR_UP)
LZ, LH, LN, LETTER = 0, 4096, 4608, 4624


def after(values, others):
    n = len(values)
    return lax.optimization_barrier((*values, *others))[:n]


def vmem_call(kernel, scalars, arrays, out_shape, scratch, flops, space=pltpu.VMEM, out_space=pltpu.VMEM):
    whole, whole_out = pl.BlockSpec(memory_space=space), pl.BlockSpec(memory_space=out_space)
    many = isinstance(out_shape, (list, tuple))
    outs = list(out_shape) if many else [out_shape]
    size = sum(a.size * a.dtype.itemsize for a in list(arrays) + outs)
    return pl.pallas_call(
        kernel,
        out_shape=out_shape,
        grid_spec=pltpu.PrefetchScalarGridSpec(
            num_scalar_prefetch=len(scalars),
            grid=(),
            in_specs=[whole] * len(arrays),
            out_specs=[whole_out] * len(outs) if many else whole_out,
            scratch_shapes=scratch,
        ),
        compiler_params=pltpu.CompilerParams(vmem_limit_bytes=VMEM_LIMIT),
        cost_estimate=pl.CostEstimate(flops=flops, bytes_accessed=size, transcendentals=0),
    )(*scalars, *arrays)


def inner_stripe(pos, dz, dyl):
    return lax.rem(pos[PZ] + dz + 4, 4) * 2 + lax.rem(pos[PYL] + dyl, 2)


def chip_of(pos, dx, dyh):
    return lax.rem(pos[PYH] + dyh, 2) * 4 + lax.rem(pos[PX] + dx + 4, 4)


def spot_of(pos, chip):
    return lax.rem(chip // 4 + pos[PYH], 2) * 4 + lax.rem(lax.rem(chip, 4) - pos[PX] + 4, 4)


def table_row(pos, chip, core, j):
    return lax.rem(core + pos[PP], 2) * 32 + spot_of(pos, chip) * 4 + j


def rows_at(start, size=B):
    return pl.ds(pl.multiple_of(start, size), size)


def coupled_kernel(pieces, first, last, table, pos, *refs):
    n = len(pieces)
    xs, rest = refs[:n], refs[n:]
    z_own, z_sib = rest[:2]
    before = None if first else rest[2]
    out, lhs, rhs = rest[-3:]
    c, p = pos[PC], pos[PP]

    def one(source, core, j):
        row = table_row(pos, c, core, j)
        live = table[row, ZN]
        for spot, (ref, (dz, dyl)) in enumerate(zip(xs, pieces)):
            t = inner_stripe(pos, dz, dyl)
            col = table[row, ZC + t] - t * 8
            lhs[:, spot * B : spot * B + B] = ref[:, rows_at(col * B)]
            block = source[t, rows_at(j * B), :]
            rhs[:, spot * B : spot * B + B] = jnp.where(t < live, block, jnp.zeros_like(block))
        total = lax.dot_general(lhs[...], rhs[...], (((1,), (1,)), ((), ())), preferred_element_type=F32)
        here = rows_at((core * 4 + j) * B)
        if not first:
            total += before[:, here]
        out[:, here] = total.astype(out.dtype)

    @pl.loop(0, 4)
    def _(j):
        one(z_own, p, j)
        one(z_sib, 1 - p, j)


def x_out_kernel(pieces, first, last, table, pos, *refs):
    n = len(pieces)
    blocks, rest = refs[:n], refs[n:]
    sources, outs = rest[:2], rest[-3:-1]
    befores = (None, None) if first else rest[2:4]
    acc = rest[-1]
    p, m = pos[PP], pos[PM]
    for source, out, before, core in zip(sources, outs, befores, (p, 1 - p)):
        acc[...] = jnp.zeros_like(acc) if first else before[...]

        @pl.loop(0, 4)
        def _(i):
            row = table_row(pos, m, core, i)
            live = table[row, ZN]
            for ref, (dx, dyh) in zip(blocks, pieces):
                t = chip_of(pos, dx, dyh)
                q = table[row, ZC + t] - t * 8 - p * 4

                @pl.when((t < live) & (q >= 0) & (q < 4))
                def _():
                    acc[rows_at(i * B), :] += jnp.dot(source[i, t], ref[rows_at(q * B), :], preferred_element_type=F32)

        out[...] = acc[...].astype(out.dtype)


def pick_kernel(pos, *refs):
    letters, (stripe, slots, sems) = refs[:8], refs[8:]
    c = pos[PC]
    row = pl.ds(pl.multiple_of(c * 512, 512), 512)
    copies = [pltpu.make_async_copy(v.at[row], slots.at[n], sems.at[n]) for n, v in enumerate(letters)]
    for copy in copies:
        copy.start()
    for v, (dx, dyh) in zip(letters, GATHERED):

        @pl.when(chip_of(pos, dx, dyh) == c)
        def _():
            copy = pltpu.make_async_copy(v.at[pl.ds(0, 4096)], stripe, sems.at[8])
            copy.start()
            copy.wait()

    for copy in copies:
        copy.wait()


def w_kernel(table, pos, *refs):
    letters, (mine, theirs, z_m, h_c, acc, sems) = refs[:8], refs[8:]
    p, m, c = pos[PP], pos[PM], pos[PC]
    row = pl.ds(pl.multiple_of(m * 512, 512), 512)
    copies = []
    for n, v in enumerate(letters):
        copies.append(pltpu.make_async_copy(v.at[row], z_m.at[n], sems.at[0, n]))
        copies.append(pltpu.make_async_copy(v.at[pl.ds(LH, 512)], h_c.at[n], sems.at[1, n]))
    for copy in copies:
        copy.start()
    acc[...] = jnp.zeros_like(acc)
    for n in range(8):
        copies[2 * n].wait()
        copies[2 * n + 1].wait()

        @pl.loop(0, 4)
        def _(j):
            row = n * 4 + j
            i = table[row, ZC + m] - m * 8
            col = table[row, HC + c] - c * 8

            @pl.when((m < table[row, ZN]) & (c < table[row, HN]))
            def _():
                term = lax.dot_general(
                    z_m[n, rows_at(j * B), :],
                    h_c[n, rows_at(j * B), :],
                    (((0,), (0,)), ((), ())),
                    preferred_element_type=F32,
                )
                acc[rows_at(i * B), rows_at(col * B)] += term

    mine[...] = acc[rows_at(p * 512, 512), :]
    theirs[...] = acc[rows_at(512 - p * 512, 512), :].astype(BF)


def h_perp_kernel(pieces, first, last, table, pos, *refs):
    n = len(pieces)
    blocks, rest = refs[:n], refs[n:]
    own, sib = rest[:2]
    out, acc = rest[-2:]
    c, p = pos[PC], pos[PP]
    acc[...] = jnp.zeros_like(acc) if first else rest[2][...]

    @pl.loop(0, 4)
    def _(j):
        for source, core in ((own, p), (sib, 1 - p)):
            for ref, (dz, dyl) in zip(blocks, pieces):
                t = inner_stripe(pos, dz, dyl)
                row = table_row(pos, t, core, j)
                col = table[row, ZC + c] - c * 8

                @pl.when(c < table[row, ZN])
                def _():
                    term = jnp.dot(
                        ref[:, rows_at((core * 4 + j) * B)],
                        source[spot_of(pos, t), rows_at(j * B), :],
                        preferred_element_type=F32,
                    )
                    acc[:, rows_at(col * B)] += term

    out[...] = acc[...].astype(out.dtype)


def part(kernel, scalars, blocks, fixed, before, last, outs, scratch):
    pieces = tuple(blocks)
    shapes = [jax.ShapeDtypeStruct((512, 1024), t) for t in outs]
    got = vmem_call(
        functools.partial(kernel, pieces, not before, last),
        scalars,
        (*blocks.values(), *fixed, *before),
        shapes,
        scratch,
        2 * 8 * len(pieces) * 512 * B * B,
    )
    return list(got)


def body(h_blocks, h_cols, h_count, z_blocks, z_cols, z_count, x_perp):
    r, c = lax.axis_index("rows"), lax.axis_index("inner")
    m, p = r // 2, r % 2
    yh, x, z, yl = m // 4, m % 4, c // 2, c % 2
    pos = jnp.stack([x, yh, p, z, yl, m, c, r]).astype(jnp.int32)
    up_z, down_z, up_x, down_x = along_z(1), along_z(-1), along_x(1), along_x(-1)

    names = jnp.concatenate([z_cols, h_cols, z_count[:, None], h_count[:, None]], axis=1)
    names = jnp.pad(names.astype(BF), ((0, 12), (0, 110)))
    h_c = lax.dynamic_index_in_dim(h_blocks, c, 1, keepdims=False).reshape(512, B)
    l = jnp.concatenate([z_blocks.transpose(1, 0, 2, 3).reshape(4096, B), h_c, names], axis=0)

    xa, xb = send(x_perp, up_z), send(x_perp, down_z)
    la, lb, ly = send(l, up_x), send(l, down_x), send(l, other_yh)
    la_, ly_, x_, xa_ = after((la, ly, x_perp, xa), (lb, xb))
    la2, lyb = send(la_, up_x), send(ly_, down_x)
    xy, xa2 = send(x_, other_yl), send(xa_, up_z)
    ly_, lyb_, xy_, xa2_ = after((ly, lyb, xy, xa2), (la2,))
    lya, lyb2 = send(ly_, up_x), send(lyb_, down_x)
    xya, xyb, xya2 = send(xy_, up_z), send(xy_, down_z), send(xa2_, other_yl)

    lya, lyb2 = after((lya, lyb2), (xya, xyb, xya2))
    came = {OWN: l, UP: la, DOWN: lb, PAIR: ly, FAR: la2, PAIR_UP: lya, PAIR_DOWN: lyb, PAIR_FAR: lyb2}
    letters = [came[at] for at in GATHERED]
    table = jnp.concatenate([v[LN : LN + 4, :18] for v in letters], axis=0).astype(jnp.int32)
    table = jnp.concatenate([table, send(table, other_core)], axis=0)
    at = (table, pos)
    tile = jax.ShapeDtypeStruct((512, 1024), BF)
    wide = pltpu.VMEM((512, 1024), F32)
    slot = jax.ShapeDtypeStruct((8, 512, B), BF)
    z_stripe, slots_zc = vmem_call(
        pick_kernel,
        (pos,),
        letters,
        [jax.ShapeDtypeStruct((4096, B), BF), slot],
        [pltpu.SemaphoreType.DMA((9,))],
        0,
        pl.ANY,
        pl.ANY,
    )
    z_stripe = z_stripe.reshape(8, 512, B)
    z_stripe_sib = send(z_stripe, other_core)
    slots_zc_sib = send(slots_zc, other_core)
    z_sib = send(z_blocks, other_core)
    w_mine, w_theirs = vmem_call(
        w_kernel,
        at,
        letters,
        [jax.ShapeDtypeStruct((512, 1024), F32), tile],
        [pltpu.VMEM((8, 512, B), BF)] * 2 + [pltpu.VMEM((1024, 1024), F32), pltpu.SemaphoreType.DMA((2, 8))],
        64 * 2 * B**3,
        pl.ANY,
    )
    w = (w_mine + send(w_theirs, other_core).astype(F32)).astype(BF)
    z_c_rows = (z_stripe, z_stripe_sib)

    def coupled_part(blocks, before, last):
        n = len(blocks) * B
        scratch = [pltpu.VMEM((512, n), BF), pltpu.VMEM((B, n), BF)]
        return part(coupled_kernel, at, blocks, z_c_rows, before, last, [BF if last else F32], scratch)

    x_all = {OWN: x_perp, UP: xa, DOWN: xb, PAIR: xy, FAR: xa2, PAIR_UP: xya, PAIR_DOWN: xyb, PAIR_FAR: xya2}
    (v,) = coupled_part(x_all, [], True)

    v_, w_ = after((v, w), (slots_zc_sib, z_sib))
    va, vb, vy = send(v_, up_x), send(v_, down_x), send(v_, other_yh)
    wa, wb = send(w_, up_z), send(w_, down_z)
    va_, vy_, w_, wa_ = after((va, vy, w, wa), (vb, wb))
    va2, vyb = send(va_, up_x), send(vy_, down_x)
    wy, wa2 = send(w_, other_yl), send(wa_, up_z)
    def x_part(blocks, before, last):
        return part(
            x_out_kernel, at, blocks, (z_blocks, z_sib), before, last, [F32, BF] if last else [F32, F32], [wide]
        )

    def h_part(blocks, before, last):
        return part(h_perp_kernel, at, blocks, (slots_zc, slots_zc_sib), before, last, [BF if last else F32], [wide])

    vy_, vyb_, wy_, wa2_ = after((vy, vyb, wy, wa2), (va2,))
    vya, vyb2 = send(vy_, up_x), send(vyb_, down_x)
    wya, wyb, wya2 = send(wy_, up_z), send(wy_, down_z), send(wa2_, other_yl)
    xs = x_part({OWN: v, UP: va, DOWN: vb, PAIR: vy, FAR: va2, PAIR_DOWN: vyb}, [], False)
    hs = h_part({OWN: w, UP: wa, DOWN: wb, PAIR: wy, FAR: wa2}, [], False)
    mine, theirs = x_part({PAIR_UP: vya, PAIR_FAR: vyb2}, xs, True)
    x_tile = (mine + send(theirs, other_core).astype(F32)).astype(BF)
    (h_tile,) = h_part({PAIR_UP: wya, PAIR_DOWN: wyb, PAIR_FAR: wya2}, hs, True)
    return h_tile, x_tile


def solution(mesh):
    in_specs = (
        P("rows", None, None, None),
        P("rows", None),
        P("rows"),
        P("rows", None, None, None),
        P("rows", None),
        P("rows"),
        P("rows", "inner"),
    )
    out_specs = (P("rows", "inner"), P("rows", "inner"))
    return jax.shard_map(body, mesh=mesh, in_specs=in_specs, out_specs=out_specs, check_vma=False)
```

```python
import functools

import jax
import jax.numpy as jnp
from jax import lax
from jax.experimental import pallas as pl
from jax.experimental.pallas import tpu as pltpu
from jax.sharding import PartitionSpec as P

AXES = ("rows", "inner")
B = 128
BF = jnp.bfloat16
F32 = jnp.float32
MIB = 1024 * 1024
ZC, HC, ZN, HN = 0, 8, 4, 5
PX, PYH, PP, PZ, PYL, PM, PC, PR = range(8)


def places():
    for yh in range(2):
        for x in range(4):
            for p in range(2):
                for z in range(4):
                    for yl in range(2):
                        yield yh, x, p, z, yl


def number(yh, x, p, z, yl):
    return (((yh * 4 + x % 4) * 2 + p) * 4 + z % 4) * 2 + yl


def send(value, to):
    return lax.ppermute(value, AXES, [(number(*at), number(*to(*at))) for at in places()])


def along_x(d):
    return lambda yh, x, p, z, yl: (yh, (x + d) % 4, p, z, yl)


def along_z(d):
    return lambda yh, x, p, z, yl: (yh, x, p, (z + d) % 4, yl)


def other_yh(yh, x, p, z, yl):
    return 1 - yh, x, p, z, yl


def other_yl(yh, x, p, z, yl):
    return yh, x, p, z, 1 - yl


def other_core(yh, x, p, z, yl):
    return yh, x, 1 - p, z, yl


OWN, UP, DOWN, FAR = (0, 0), (-1, 0), (1, 0), (2, 0)
PAIR, PAIR_UP, PAIR_DOWN, PAIR_FAR = (0, 1), (-1, 1), (1, 1), (2, 1)
GATHERED = (OWN, DOWN, FAR, UP, PAIR, PAIR_DOWN, PAIR_FAR, PAIR_UP)
LZ, LH, LN, LETTER = 0, 4096, 4608, 4624


def after(*values):
    return lax.optimization_barrier(values)


def in_hbm(value):
    return pltpu.with_memory_space_constraint(value, pltpu.HBM)


def vmem_call(kernel, scalars, arrays, out_shape, scratch, flops, mib, space=pltpu.VMEM, out_space=pltpu.VMEM):
    spaces = space if isinstance(space, list) else [space] * len(arrays)
    whole_out = pl.BlockSpec(memory_space=out_space)
    many = isinstance(out_shape, (list, tuple))
    outs = list(out_shape) if many else [out_shape]
    size = sum(a.size * a.dtype.itemsize for a in list(arrays) + outs)
    return pl.pallas_call(
        kernel,
        out_shape=out_shape,
        grid_spec=pltpu.PrefetchScalarGridSpec(
            num_scalar_prefetch=len(scalars),
            grid=(),
            in_specs=[pl.BlockSpec(memory_space=v) for v in spaces],
            out_specs=[whole_out] * len(outs) if many else whole_out,
            scratch_shapes=scratch,
        ),
        compiler_params=pltpu.CompilerParams(vmem_limit_bytes=mib * MIB),
        cost_estimate=pl.CostEstimate(flops=flops, bytes_accessed=size, transcendentals=0),
    )(*scalars, *arrays)


def inner_stripe(pos, dz, dyl):
    return lax.rem(pos[PZ] + dz + 4, 4) * 2 + lax.rem(pos[PYL] + dyl, 2)


def chip_of(pos, dx, dyh):
    return lax.rem(pos[PYH] + dyh, 2) * 4 + lax.rem(pos[PX] + dx + 4, 4)


def spot_of(pos, chip):
    return lax.rem(chip // 4 + pos[PYH], 2) * 4 + lax.rem(lax.rem(chip, 4) - pos[PX] + 4, 4)


class Row:
    def __init__(self, table, side, piece, j):
        self.table, self.side, self.piece, self.j = table, side, piece, j

    def z_name(self, t):
        return self.table[self.side, self.piece, self.j, ZC + t]

    def h_name(self, s):
        return self.table[self.side, self.piece, self.j, HC + s]

    def z_live(self, t):
        return t < self.table[self.side, self.piece, ZN, self.j]

    def h_live(self, s):
        return s < self.table[self.side, self.piece, HN, self.j]


def rows_at(start, size=B):
    return pl.ds(pl.multiple_of(start, size), size)


def masked(live, block):
    return jnp.where(live, block, jnp.zeros_like(block))


def pick_kernel(pos, *refs):
    letters, (stripe, slots, names, sems) = refs[:8], refs[8:]
    c = pos[PC]
    copies = []
    for n, v in enumerate(letters):
        copies.append(pltpu.make_async_copy(v.at[rows_at(c * 512, 512)], slots.at[n], sems.at[0, n]))
        copies.append(pltpu.make_async_copy(v.at[pl.ds(LN, 16)], names.at[n], sems.at[1, n]))
    for copy in copies:
        copy.start()
    for v, (dx, dyh) in zip(letters, GATHERED):

        @pl.when(chip_of(pos, dx, dyh) == c)
        def _():
            copy = pltpu.make_async_copy(v.at[pl.ds(0, 4096)], stripe, sems.at[2, 0])
            copy.start()
            copy.wait()

    for copy in copies:
        copy.wait()


def coupled_kernel(pieces, table, pos, *refs):
    xs, (z_own, z_sib, out) = refs[:8], refs[8:]
    c, p = pos[PC], pos[PP]
    stripes = [inner_stripe(pos, dz, dyl) for dz, dyl in pieces]
    for side, (source, core) in enumerate(((z_own, p), (z_sib, 1 - p))):
        for j in range(4):
            row = Row(table, side, spot_of(pos, c), j)
            total = None
            for n in range(0, 8, 2):
                lhs, rhs = [], []
                for ref, t in zip(xs[n : n + 2], stripes[n : n + 2]):
                    lhs.append(ref[:, rows_at((row.z_name(t) - t * 8) * B)])
                    rhs.append(masked(row.z_live(t), source[rows_at(t * 512 + j * B), :]))
                term = lax.dot_general(
                    jnp.concatenate(lhs, axis=1),
                    jnp.concatenate(rhs, axis=1),
                    (((1,), (1,)), ((), ())),
                    preferred_element_type=F32,
                )
                total = term if total is None else total + term
            out[:, rows_at((core * 4 + j) * B)] = total.astype(BF)


def x_out_kernel(pieces, first, last, table, pos, *refs):
    n = len(pieces)
    blocks, rest = refs[:n], refs[n:]
    z_own, z_sib = rest[:2]
    befores = None if first else rest[2:4]
    mine, theirs, z, held, sems = rest[-5:]
    p, m = pos[PP], pos[PM]
    copies = [pltpu.make_async_copy(v, held.at[pl.ds(s * 512, 512)], sems.at[s]) for s, v in enumerate(blocks)]
    for copy in copies:
        copy.start()
    for s, (dx, dyh) in enumerate(pieces):
        t = chip_of(pos, dx, dyh)
        for side, source in enumerate((z_own, z_sib)):
            for i in range(4):
                row = Row(table, side, 0, i)
                q = row.z_name(t) - t * 8 - p * 4
                block = masked(row.z_live(t), source[i, t])
                for k in range(4):
                    at = (side * 4 + i) * B, (s * 4 + k) * B
                    z[at[0] : at[0] + B, at[1] : at[1] + B] = masked(q == k, block)
    for copy in copies:
        copy.wait()
    for side, out in enumerate((mine, theirs)):
        total = jnp.dot(z[side * 512 : side * 512 + 512, :], held[...], preferred_element_type=F32)
        if not first:
            total += befores[side][...].astype(F32)
        out[...] = total.astype(out.dtype)


def w_kernel(spots, first, last, table, pos, *refs):
    n = len(spots)
    letters, rest = refs[:n], refs[n:]
    before = None if first else rest[0]
    z_m, h_c, acc, sems = rest[-4:]
    p, m, c = pos[PP], pos[PM], pos[PC]
    copies = []
    for s, v in enumerate(letters):
        copies.append(pltpu.make_async_copy(v.at[rows_at(m * 512, 512)], z_m.at[s], sems.at[0, s]))
        copies.append(pltpu.make_async_copy(v.at[pl.ds(LH, 512)], h_c.at[s], sems.at[1, s]))
    for copy in copies:
        copy.start()
    acc[...] = jnp.zeros_like(acc) if first else before[...]
    for copy in copies:
        copy.wait()
    for s, spot in enumerate(spots):
        for j in range(4):
            row = Row(table, 0, spot, j)
            i = row.z_name(m) - m * 8
            col = row.h_name(c) - c * 8
            term = lax.dot_general(
                masked(row.z_live(m) & row.h_live(c), z_m[s, j * B : j * B + B, :]),
                h_c[s, j * B : j * B + B, :],
                (((0,), (0,)), ((), ())),
                preferred_element_type=F32,
            )
            acc[rows_at(i * B), rows_at(col * B)] += term

    if last:
        mine, theirs = rest[-6:-4]
        mine[...] = acc[rows_at(p * 512, 512), :]
        theirs[...] = acc[rows_at(512 - p * 512, 512), :].astype(BF)
    else:
        rest[-5][...] = acc[...]


def h_perp_kernel(pieces, first, last, table, pos, *refs):
    n = len(pieces)
    blocks, rest = refs[:n], refs[n:]
    own, sib = rest[:2]
    out, acc = rest[-2:]
    c, p = pos[PC], pos[PP]
    acc[...] = jnp.zeros_like(acc) if first else rest[2][...].astype(F32)
    for ref, (dz, dyl) in zip(blocks, pieces):
        spot = spot_of(pos, inner_stripe(pos, dz, dyl))
        for side, (source, core) in enumerate(((own, p), (sib, 1 - p))):
            for j in range(4):
                row = Row(table, side, spot, j)
                term = jnp.dot(
                    ref[:, rows_at((core * 4 + j) * B)],
                    masked(row.z_live(c), source[spot, j * B : j * B + B, :]),
                    preferred_element_type=F32,
                )
                acc[:, rows_at((row.z_name(c) - c * 8) * B)] += term
    out[...] = acc[...].astype(out.dtype)


def part(kernel, scalars, blocks, fixed, before, last, outs, scratch, mib, space=pltpu.VMEM):
    pieces = tuple(blocks)
    shapes = [jax.ShapeDtypeStruct((512, 1024), t) for t in outs]
    got = vmem_call(
        functools.partial(kernel, pieces, not before, last),
        scalars,
        (*blocks.values(), *fixed, *before),
        shapes,
        scratch,
        2 * 8 * len(pieces) * 512 * B * B,
        mib,
        [space] * len(pieces) + [pltpu.VMEM] * (len(fixed) + len(before)),
    )
    return list(got)


def body(h_blocks, h_cols, h_count, z_blocks, z_cols, z_count, x_perp):
    r, c = lax.axis_index("rows"), lax.axis_index("inner")
    m, p = r // 2, r % 2
    yh, ax, az, yl = m // 4, m % 4, c // 2, c % 2
    pos = jnp.stack([ax, yh, p, az, yl, m, c, r]).astype(jnp.int32)
    up_z, down_z, up_x, down_x = along_z(1), along_z(-1), along_x(1), along_x(-1)

    def at_place(v, row, column):
        return jnp.pad(v, ((row, 16 - row - v.shape[0]), (column, B - column - v.shape[1])))

    names = at_place(z_cols, 0, ZC) + at_place(h_cols, 0, HC)
    names = names + at_place(z_count[None, :], ZN, 0) + at_place(h_count[None, :], HN, 0)
    h_c = lax.dynamic_index_in_dim(h_blocks, c, 1, keepdims=False).reshape(512, B)
    z_slots = z_blocks.transpose(1, 0, 2, 3).reshape(4096, B)
    l = jnp.concatenate([z_slots, h_c, names.astype(BF)], axis=0)

    la, lb, ly = send(l, up_x), send(l, down_x), send(l, other_yh)
    xa, xb = send(x_perp, up_z), send(x_perp, down_z)
    l, la, lb, ly, x, xa, xb, z = after(l, la, lb, ly, x_perp, xa, xb, z_blocks)
    la2, lyb = send(la, up_x), send(ly, down_x)
    xy, xa2 = send(x, other_yl), send(xa, up_z)
    z_sib = send(z, other_core)
    la2, ly, lyb, xy, xa2, z_sib = after(la2, ly, lyb, xy, xa2, z_sib)
    lya, lyb2 = send(ly, up_x), send(lyb, down_x)
    xya, xyb, xya2 = send(xy, up_z), send(xy, down_z), send(xa2, other_yl)

    tile = jax.ShapeDtypeStruct((512, 1024), BF)

    def table_of(letters):
        return jnp.stack([v[LN : LN + 6, :16] for v in letters]).astype(jnp.int32)

    def w_part(letters, names, before, last):
        shapes = [jax.ShapeDtypeStruct((512, 1024), F32), tile] if last else [jax.ShapeDtypeStruct((1024, 1024), F32)]
        n = len(letters)
        scratch = [pltpu.VMEM((n, 512, B), BF)] * 2 + [pltpu.VMEM((1024, 1024), F32), pltpu.SemaphoreType.DMA((2, n))]
        spaces = [pl.ANY] * n + [pltpu.VMEM] * len(before)
        arrays = (*[in_hbm(v) for v in letters.values()], *before)
        kernel = functools.partial(w_kernel, tuple(letters), not before, last)
        return list(vmem_call(kernel, (names, pos), arrays, shapes, scratch, 8 * n * B**3, 22, spaces))

    early = {0: l, 1: lb, 2: la2, 3: la, 4: ly, 5: lyb}
    names_early = table_of([*early.values(), l, l])[None]
    ws = w_part(early, names_early, [], False)
    lya, lyb2, xya, xyb, xya2, *ws = after(lya, lyb2, xya, xyb, xya2, *ws)

    letters = [*early.values(), lyb2, lya]
    z_stripe, slots_zc, names = vmem_call(
        pick_kernel,
        (pos,),
        [in_hbm(v) for v in letters],
        [jax.ShapeDtypeStruct((*n, B), BF) for n in ((4096,), (8, 512), (8, 16))],
        [pltpu.SemaphoreType.DMA((3, 8))],
        0,
        2,
        pl.ANY,
        pl.ANY,
    )
    table = names[:, :6, :16].astype(jnp.int32)
    table = jnp.stack([table, send(table, other_core)])
    at = (table, pos)
    z_stripe_sib = send(z_stripe, other_core)
    w_mine, w_theirs = w_part({6: lyb2, 7: lya}, table, ws, True)
    w = (w_mine + send(w_theirs, other_core).astype(F32)).astype(BF)
    x_all = {OWN: x, UP: xa, DOWN: xb, PAIR: xy, FAR: xa2, PAIR_UP: xya, PAIR_DOWN: xyb, PAIR_FAR: xya2}
    v = vmem_call(
        functools.partial(coupled_kernel, tuple(x_all)),
        at,
        (*x_all.values(), z_stripe, z_stripe_sib),
        tile,
        [],
        2 * 64 * 512 * B * B,
        18,
    )

    v, w = after(v, w)
    va, vb, vy = send(v, up_x), send(v, down_x), send(v, other_yh)
    wa, wb = send(w, up_z), send(w, down_z)
    va, vb, vy, wa, wb, w, slots_zc = after(va, vb, vy, wa, wb, w, slots_zc)
    va2, vyb = send(va, up_x), send(vy, down_x)
    wy, wa2 = send(w, other_yl), send(wa, up_z)
    slots_zc_sib = send(slots_zc, other_core)

    def x_part(blocks, before, last):
        n = len(blocks)
        scratch = [pltpu.VMEM((1024, 512 * n), BF), pltpu.VMEM((512 * n, 1024), BF), pltpu.SemaphoreType.DMA((n,))]
        outs = [F32, BF] if last else [BF, BF]
        return part(x_out_kernel, at, blocks, (z, z_sib), before, last, outs, scratch, 14 + 3 * n, pl.ANY)

    def h_part(blocks, before, last):
        scratch = [pltpu.VMEM((512, 1024), F32)]
        return part(h_perp_kernel, at, blocks, (slots_zc, slots_zc_sib), before, last, [BF], scratch, 12 + len(blocks))

    va2, vy, vyb, wy, wa2, slots_zc_sib = after(va2, vy, vyb, wy, wa2, slots_zc_sib)
    vya, vyb2 = send(vy, up_x), send(vyb, down_x)
    wya, wyb, wya2 = send(wy, up_z), send(wy, down_z), send(wa2, other_yl)
    xs = x_part({OWN: v, UP: va, DOWN: vb, PAIR: vy, FAR: va2, PAIR_DOWN: vyb}, [], False)
    hs = h_part({OWN: w, UP: wa, DOWN: wb, PAIR: wy, FAR: wa2}, [], False)
    vya, vyb2, *hs = after(vya, vyb2, *hs)
    mine, theirs = x_part({PAIR_UP: vya, PAIR_FAR: vyb2}, xs, True)
    x_tile = (mine + send(theirs, other_core).astype(F32)).astype(BF)
    (h_tile,) = h_part({PAIR_UP: wya, PAIR_DOWN: wyb, PAIR_FAR: wya2}, hs, True)
    return h_tile, x_tile


def solution(mesh):
    in_specs = (
        P("rows", None, None, None),
        P("rows", None),
        P("rows"),
        P("rows", None, None, None),
        P("rows", None),
        P("rows"),
        P("rows", "inner"),
    )
    out_specs = (P("rows", "inner"), P("rows", "inner"))
    return jax.shard_map(body, mesh=mesh, in_specs=in_specs, out_specs=out_specs, check_vma=False)
```

```python
import functools

import jax
import jax.numpy as jnp
from jax import lax
from jax.experimental import pallas as pl
from jax.experimental.pallas import tpu as pltpu
from jax.sharding import PartitionSpec as P

AXES = ("rows", "inner")
B = 128
BF = jnp.bfloat16
F32 = jnp.float32
MIB = 1024 * 1024
ZC, HC, ZN, HN = 0, 8, 4, 5
PX, PYH, PP, PZ, PYL, PM, PC, PR = range(8)


def places():
    for yh in range(2):
        for x in range(4):
            for p in range(2):
                for z in range(4):
                    for yl in range(2):
                        yield yh, x, p, z, yl


def number(yh, x, p, z, yl):
    return (((yh * 4 + x % 4) * 2 + p) * 4 + z % 4) * 2 + yl


def send(value, to):
    return lax.ppermute(value, AXES, [(number(*at), number(*to(*at))) for at in places()])


def along_x(d):
    return lambda yh, x, p, z, yl: (yh, (x + d) % 4, p, z, yl)


def along_z(d):
    return lambda yh, x, p, z, yl: (yh, x, p, (z + d) % 4, yl)


def other_yh(yh, x, p, z, yl):
    return 1 - yh, x, p, z, yl


def other_yl(yh, x, p, z, yl):
    return yh, x, p, z, 1 - yl


def other_core(yh, x, p, z, yl):
    return yh, x, 1 - p, z, yl


OWN, UP, DOWN, FAR = (0, 0), (-1, 0), (1, 0), (2, 0)
PAIR, PAIR_UP, PAIR_DOWN, PAIR_FAR = (0, 1), (-1, 1), (1, 1), (2, 1)
GATHERED = (OWN, DOWN, FAR, UP, PAIR, PAIR_DOWN, PAIR_FAR, PAIR_UP)
LZ, LH, LN, LETTER = 0, 4096, 4608, 4624


def after(*values):
    return lax.optimization_barrier(values)


def in_hbm(value):
    return pltpu.with_memory_space_constraint(value, pltpu.HBM)


def vmem_call(kernel, scalars, arrays, out_shape, scratch, flops, mib, space=pltpu.VMEM, out_space=pltpu.VMEM):
    spaces = space if isinstance(space, list) else [space] * len(arrays)
    whole_out = pl.BlockSpec(memory_space=out_space)
    many = isinstance(out_shape, (list, tuple))
    outs = list(out_shape) if many else [out_shape]
    size = sum(a.size * a.dtype.itemsize for a in list(arrays) + outs)
    return pl.pallas_call(
        kernel,
        out_shape=out_shape,
        grid_spec=pltpu.PrefetchScalarGridSpec(
            num_scalar_prefetch=len(scalars),
            grid=(),
            in_specs=[pl.BlockSpec(memory_space=v) for v in spaces],
            out_specs=[whole_out] * len(outs) if many else whole_out,
            scratch_shapes=scratch,
        ),
        compiler_params=pltpu.CompilerParams(vmem_limit_bytes=mib * MIB),
        cost_estimate=pl.CostEstimate(flops=flops, bytes_accessed=size, transcendentals=0),
    )(*scalars, *arrays)


def inner_stripe(pos, dz, dyl):
    return lax.rem(pos[PZ] + dz + 4, 4) * 2 + lax.rem(pos[PYL] + dyl, 2)


def chip_of(pos, dx, dyh):
    return lax.rem(pos[PYH] + dyh, 2) * 4 + lax.rem(pos[PX] + dx + 4, 4)


def spot_of(pos, chip):
    return lax.rem(chip // 4 + pos[PYH], 2) * 4 + lax.rem(lax.rem(chip, 4) - pos[PX] + 4, 4)


class Row:
    def __init__(self, table, side, piece, j):
        self.table, self.side, self.piece, self.j = table, side, piece, j

    def z_name(self, t):
        return self.table[self.side, self.piece, self.j, ZC + t]

    def h_name(self, s):
        return self.table[self.side, self.piece, self.j, HC + s]

    def z_live(self, t):
        return t < self.table[self.side, self.piece, ZN, self.j]

    def h_live(self, s):
        return s < self.table[self.side, self.piece, HN, self.j]


def rows_at(start, size=B):
    return pl.ds(pl.multiple_of(start, size), size)


def masked(live, block):
    return jnp.where(live, block, jnp.zeros_like(block))


def pick_kernel(pos, *refs):
    letters, (stripe, slots, names, sems) = refs[:8], refs[8:]
    c = pos[PC]
    copies = []
    for n, v in enumerate(letters):
        copies.append(pltpu.make_async_copy(v.at[rows_at(c * 512, 512)], slots.at[n], sems.at[0, n]))
        copies.append(pltpu.make_async_copy(v.at[pl.ds(LN, 16)], names.at[n], sems.at[1, n]))
    for copy in copies:
        copy.start()
    for v, (dx, dyh) in zip(letters, GATHERED):

        @pl.when(chip_of(pos, dx, dyh) == c)
        def _():
            copy = pltpu.make_async_copy(v.at[pl.ds(0, 4096)], stripe, sems.at[2, 0])
            copy.start()
            copy.wait()

    for copy in copies:
        copy.wait()


def coupled_kernel(pieces, table, pos, *refs):
    xs, (z_own, z_sib, out) = refs[:8], refs[8:]
    c, p = pos[PC], pos[PP]
    stripes = [inner_stripe(pos, dz, dyl) for dz, dyl in pieces]
    for side, (source, core) in enumerate(((z_own, p), (z_sib, 1 - p))):
        for j in range(4):
            row = Row(table, side, spot_of(pos, c), j)
            total = None
            for n in range(0, 8, 2):
                lhs, rhs = [], []
                for ref, t in zip(xs[n : n + 2], stripes[n : n + 2]):
                    lhs.append(ref[:, rows_at((row.z_name(t) - t * 8) * B)])
                    rhs.append(masked(row.z_live(t), source[rows_at(t * 512 + j * B), :]))
                term = lax.dot_general(
                    jnp.concatenate(lhs, axis=1),
                    jnp.concatenate(rhs, axis=1),
                    (((1,), (1,)), ((), ())),
                    preferred_element_type=F32,
                )
                total = term if total is None else total + term
            out[:, rows_at((core * 4 + j) * B)] = total.astype(BF)


def x_out_kernel(pieces, first, last, table, pos, *refs):
    n = len(pieces)
    blocks, rest = refs[:n], refs[n:]
    z_own, z_sib = rest[:2]
    befores = None if first else rest[2:4]
    mine, theirs, z, held, sems = rest[-5:]
    p, m = pos[PP], pos[PM]
    copies = [pltpu.make_async_copy(v, held.at[pl.ds(s * 512, 512)], sems.at[s]) for s, v in enumerate(blocks)]
    for copy in copies:
        copy.start()
    for s, (dx, dyh) in enumerate(pieces):
        t = chip_of(pos, dx, dyh)
        for side, source in enumerate((z_own, z_sib)):
            for i in range(4):
                row = Row(table, side, 0, i)
                q = row.z_name(t) - t * 8 - p * 4
                block = masked(row.z_live(t), source[i, t])
                for k in range(4):
                    at = (side * 4 + i) * B, (s * 4 + k) * B
                    z[at[0] : at[0] + B, at[1] : at[1] + B] = masked(q == k, block)
    for copy in copies:
        copy.wait()
    for side, out in enumerate((mine, theirs)):
        total = jnp.dot(z[side * 512 : side * 512 + 512, :], held[...], preferred_element_type=F32)
        if not first:
            total += befores[side][...].astype(F32)
        out[...] = total.astype(out.dtype)


def w_kernel(spots, first, last, table, pos, *refs):
    n = len(spots)
    letters, rest = refs[:n], refs[n:]
    before = None if first else rest[0]
    z_m, h_c, acc, sems = rest[-4:]
    p, m, c = pos[PP], pos[PM], pos[PC]
    copies = []
    for s, v in enumerate(letters):
        copies.append(pltpu.make_async_copy(v.at[rows_at(m * 512, 512)], z_m.at[s], sems.at[0, s]))
        copies.append(pltpu.make_async_copy(v.at[pl.ds(LH, 512)], h_c.at[s], sems.at[1, s]))
    for copy in copies:
        copy.start()
    acc[...] = jnp.zeros_like(acc) if first else before[...]
    for copy in copies:
        copy.wait()
    for s, spot in enumerate(spots):
        for j in range(4):
            row = Row(table, 0, spot, j)
            i = row.z_name(m) - m * 8
            col = row.h_name(c) - c * 8
            term = lax.dot_general(
                masked(row.z_live(m) & row.h_live(c), z_m[s, j * B : j * B + B, :]),
                h_c[s, j * B : j * B + B, :],
                (((0,), (0,)), ((), ())),
                preferred_element_type=F32,
            )
            acc[rows_at(i * B), rows_at(col * B)] += term

    if last:
        mine, theirs = rest[-6:-4]
        mine[...] = acc[rows_at(p * 512, 512), :]
        theirs[...] = acc[rows_at(512 - p * 512, 512), :].astype(BF)
    else:
        rest[-5][...] = acc[...]


def h_perp_kernel(pieces, first, last, table, pos, *refs):
    n = len(pieces)
    blocks, rest = refs[:n], refs[n:]
    own, sib = rest[:2]
    out, acc = rest[-2:]
    c, p = pos[PC], pos[PP]
    acc[...] = jnp.zeros_like(acc) if first else rest[2][...].astype(F32)
    for ref, (dz, dyl) in zip(blocks, pieces):
        spot = spot_of(pos, inner_stripe(pos, dz, dyl))
        for side, (source, core) in enumerate(((own, p), (sib, 1 - p))):
            for j in range(4):
                row = Row(table, side, spot, j)
                term = jnp.dot(
                    ref[:, rows_at((core * 4 + j) * B)],
                    masked(row.z_live(c), source[spot, j * B : j * B + B, :]),
                    preferred_element_type=F32,
                )
                acc[:, rows_at((row.z_name(c) - c * 8) * B)] += term
    out[...] = acc[...].astype(out.dtype)


def part(kernel, scalars, blocks, fixed, before, last, outs, scratch, mib, space=pltpu.VMEM):
    pieces = tuple(blocks)
    shapes = [jax.ShapeDtypeStruct((512, 1024), t) for t in outs]
    got = vmem_call(
        functools.partial(kernel, pieces, not before, last),
        scalars,
        (*blocks.values(), *fixed, *before),
        shapes,
        scratch,
        2 * 8 * len(pieces) * 512 * B * B,
        mib,
        [space] * len(pieces) + [pltpu.VMEM] * (len(fixed) + len(before)),
    )
    return list(got)


def body(h_blocks, h_cols, h_count, z_blocks, z_cols, z_count, x_perp):
    r, c = lax.axis_index("rows"), lax.axis_index("inner")
    m, p = r // 2, r % 2
    yh, ax, az, yl = m // 4, m % 4, c // 2, c % 2
    pos = jnp.stack([ax, yh, p, az, yl, m, c, r]).astype(jnp.int32)
    up_z, down_z, up_x, down_x = along_z(1), along_z(-1), along_x(1), along_x(-1)

    def at_place(v, row, column):
        return jnp.pad(v, ((row, 16 - row - v.shape[0]), (column, B - column - v.shape[1])))

    names = at_place(z_cols, 0, ZC) + at_place(h_cols, 0, HC)
    names = names + at_place(z_count[None, :], ZN, 0) + at_place(h_count[None, :], HN, 0)
    h_c = lax.dynamic_index_in_dim(h_blocks, c, 1, keepdims=False).reshape(512, B)
    z_slots = z_blocks.transpose(1, 0, 2, 3).reshape(4096, B)
    l = jnp.concatenate([z_slots, h_c, names.astype(BF)], axis=0)

    la, lb, ly = send(l, up_x), send(l, down_x), send(l, other_yh)
    xa, xb = send(x_perp, up_z), send(x_perp, down_z)
    l, la, lb, ly, z = after(l, la, lb, ly, z_blocks)
    x, xa, xb = after(x_perp, xa, xb)
    la2, lyb = send(la, up_x), send(ly, down_x)
    xy, xa2 = send(x, other_yl), send(xa, up_z)
    z_sib = send(z, other_core)
    la2, ly, lyb, z_sib = after(la2, ly, lyb, z_sib)
    xy, xa2 = after(xy, xa2)
    lya, lyb2 = send(ly, up_x), send(lyb, down_x)
    xya, xyb, xya2 = send(xy, up_z), send(xy, down_z), send(xa2, other_yl)

    tile = jax.ShapeDtypeStruct((512, 1024), BF)

    def table_of(letters):
        return jnp.stack([v[LN : LN + 6, :16] for v in letters]).astype(jnp.int32)

    def w_part(letters, names, before, last):
        shapes = [jax.ShapeDtypeStruct((512, 1024), F32), tile] if last else [jax.ShapeDtypeStruct((1024, 1024), F32)]
        n = len(letters)
        scratch = [pltpu.VMEM((n, 512, B), BF)] * 2 + [pltpu.VMEM((1024, 1024), F32), pltpu.SemaphoreType.DMA((2, n))]
        spaces = [pl.ANY] * n + [pltpu.VMEM] * len(before)
        arrays = (*[v if last else in_hbm(v) for v in letters.values()], *before)
        kernel = functools.partial(w_kernel, tuple(letters), not before, last)
        return list(vmem_call(kernel, (names, pos), arrays, shapes, scratch, 8 * n * B**3, 22, spaces))

    early = {0: l, 1: lb, 2: la2, 3: la, 4: ly, 5: lyb}
    names_early = table_of([*early.values(), l, l])[None]
    ws = w_part(early, names_early, [], False)
    lya, lyb2, xya, xyb, xya2, *ws = after(lya, lyb2, xya, xyb, xya2, *ws)

    letters = [*early.values(), lyb2, lya]
    z_stripe, slots_zc, names = vmem_call(
        pick_kernel,
        (pos,),
        [*[in_hbm(v) for v in early.values()], lyb2, lya],
        [jax.ShapeDtypeStruct((*n, B), BF) for n in ((4096,), (8, 512), (8, 16))],
        [pltpu.SemaphoreType.DMA((3, 8))],
        0,
        2,
        pl.ANY,
        pl.ANY,
    )
    table = names[:, :6, :16].astype(jnp.int32)
    table = jnp.stack([table, send(table, other_core)])
    at = (table, pos)
    z_stripe_sib = send(z_stripe, other_core)
    w_mine, w_theirs = w_part({6: lyb2, 7: lya}, table, ws, True)
    w = (w_mine + send(w_theirs, other_core).astype(F32)).astype(BF)
    x_all = {OWN: x, UP: xa, DOWN: xb, PAIR: xy, FAR: xa2, PAIR_UP: xya, PAIR_DOWN: xyb, PAIR_FAR: xya2}
    v = vmem_call(
        functools.partial(coupled_kernel, tuple(x_all)),
        at,
        (*x_all.values(), z_stripe, z_stripe_sib),
        tile,
        [],
        2 * 64 * 512 * B * B,
        18,
    )

    v, w = after(v, w)
    va, vb, vy = send(v, up_x), send(v, down_x), send(v, other_yh)
    wa, wb = send(w, up_z), send(w, down_z)
    va, vb, vy = after(va, vb, vy)
    wa, wb, w, slots_zc = after(wa, wb, w, slots_zc)
    va2, vyb = send(va, up_x), send(vy, down_x)
    wy, wa2 = send(w, other_yl), send(wa, up_z)
    slots_zc_sib = send(slots_zc, other_core)

    def x_part(blocks, before, last):
        n = len(blocks)
        scratch = [pltpu.VMEM((1024, 512 * n), BF), pltpu.VMEM((512 * n, 1024), BF), pltpu.SemaphoreType.DMA((n,))]
        outs = [F32, BF] if last else [BF, BF]
        return part(x_out_kernel, at, blocks, (z, z_sib), before, last, outs, scratch, 14 + 3 * n, pl.ANY)

    def h_part(blocks, before, last):
        scratch = [pltpu.VMEM((512, 1024), F32)]
        return part(h_perp_kernel, at, blocks, (slots_zc, slots_zc_sib), before, last, [BF], scratch, 12 + len(blocks))

    va2, vy, vyb = after(va2, vy, vyb)
    wy, wa2, slots_zc_sib = after(wy, wa2, slots_zc_sib)
    vya, vyb2 = send(vy, up_x), send(vyb, down_x)
    wya, wyb, wya2 = send(wy, up_z), send(wy, down_z), send(wa2, other_yl)
    xs = x_part({OWN: v, UP: va, DOWN: vb, PAIR: vy, FAR: va2, PAIR_DOWN: vyb}, [], False)
    hs = h_part({OWN: w, UP: wa, DOWN: wb, PAIR: wy, FAR: wa2}, [], False)
    vya, vyb2, *hs = after(vya, vyb2, *hs)
    mine, theirs = x_part({PAIR_UP: vya, PAIR_FAR: vyb2}, xs, True)
    x_tile = (mine + send(theirs, other_core).astype(F32)).astype(BF)
    (h_tile,) = h_part({PAIR_UP: wya, PAIR_DOWN: wyb, PAIR_FAR: wya2}, hs, True)
    return h_tile, x_tile


def solution(mesh):
    in_specs = (
        P("rows", None, None, None),
        P("rows", None),
        P("rows"),
        P("rows", None, None, None),
        P("rows", None),
        P("rows"),
        P("rows", "inner"),
    )
    out_specs = (P("rows", "inner"), P("rows", "inner"))
    return jax.shard_map(body, mesh=mesh, in_specs=in_specs, out_specs=out_specs, check_vma=False)
```

```python
import functools

import jax
import jax.numpy as jnp
from jax import lax
from jax.experimental import pallas as pl
from jax.experimental.pallas import tpu as pltpu
from jax.sharding import PartitionSpec as P

AXES = ("rows", "inner")
B = 128
BF = jnp.bfloat16
F32 = jnp.float32
MIB = 1024 * 1024
ZC, HC, ZN, HN = 0, 8, 4, 5
PX, PYH, PP, PZ, PYL, PM, PC, PR = range(8)


def places():
    for yh in range(2):
        for x in range(4):
            for p in range(2):
                for z in range(4):
                    for yl in range(2):
                        yield yh, x, p, z, yl


def number(yh, x, p, z, yl):
    return (((yh * 4 + x % 4) * 2 + p) * 4 + z % 4) * 2 + yl


def send(value, to):
    return lax.ppermute(value, AXES, [(number(*at), number(*to(*at))) for at in places()])


def along_x(d):
    return lambda yh, x, p, z, yl: (yh, (x + d) % 4, p, z, yl)


def along_z(d):
    return lambda yh, x, p, z, yl: (yh, x, p, (z + d) % 4, yl)


def other_yh(yh, x, p, z, yl):
    return 1 - yh, x, p, z, yl


def other_yl(yh, x, p, z, yl):
    return yh, x, p, z, 1 - yl


def other_core(yh, x, p, z, yl):
    return yh, x, 1 - p, z, yl


OWN, UP, DOWN, FAR = (0, 0), (-1, 0), (1, 0), (2, 0)
PAIR, PAIR_UP, PAIR_DOWN, PAIR_FAR = (0, 1), (-1, 1), (1, 1), (2, 1)
GATHERED = (OWN, DOWN, FAR, UP, PAIR, PAIR_DOWN, PAIR_FAR, PAIR_UP)
LZ, LH, LN, LETTER = 0, 4096, 4608, 4624


def after(*values):
    return lax.optimization_barrier(values)


def in_hbm(value):
    return pltpu.with_memory_space_constraint(value, pltpu.HBM)


def vmem_call(kernel, scalars, arrays, out_shape, scratch, flops, mib, space=pltpu.VMEM, out_space=pltpu.VMEM):
    spaces = space if isinstance(space, list) else [space] * len(arrays)
    whole_out = pl.BlockSpec(memory_space=out_space)
    many = isinstance(out_shape, (list, tuple))
    outs = list(out_shape) if many else [out_shape]
    size = sum(a.size * a.dtype.itemsize for a in list(arrays) + outs)
    return pl.pallas_call(
        kernel,
        out_shape=out_shape,
        grid_spec=pltpu.PrefetchScalarGridSpec(
            num_scalar_prefetch=len(scalars),
            grid=(),
            in_specs=[pl.BlockSpec(memory_space=v) for v in spaces],
            out_specs=[whole_out] * len(outs) if many else whole_out,
            scratch_shapes=scratch,
        ),
        compiler_params=pltpu.CompilerParams(vmem_limit_bytes=mib * MIB),
        cost_estimate=pl.CostEstimate(flops=flops, bytes_accessed=size, transcendentals=0),
    )(*scalars, *arrays)


def inner_stripe(pos, dz, dyl):
    return lax.rem(pos[PZ] + dz + 4, 4) * 2 + lax.rem(pos[PYL] + dyl, 2)


def chip_of(pos, dx, dyh):
    return lax.rem(pos[PYH] + dyh, 2) * 4 + lax.rem(pos[PX] + dx + 4, 4)


def spot_of(pos, chip):
    return lax.rem(chip // 4 + pos[PYH], 2) * 4 + lax.rem(lax.rem(chip, 4) - pos[PX] + 4, 4)


class Row:
    def __init__(self, table, side, piece, j):
        self.table, self.side, self.piece, self.j = table, side, piece, j

    def z_name(self, t):
        return self.table[self.side, self.piece, self.j, ZC + t]

    def h_name(self, s):
        return self.table[self.side, self.piece, self.j, HC + s]

    def z_live(self, t):
        return t < self.table[self.side, self.piece, ZN, self.j]

    def h_live(self, s):
        return s < self.table[self.side, self.piece, HN, self.j]


def rows_at(start, size=B):
    return pl.ds(pl.multiple_of(start, size), size)


def masked(live, block):
    return jnp.where(live, block, jnp.zeros_like(block))


def pick_kernel(pos, *refs):
    letters, (stripe, slots, names, sems) = refs[:8], refs[8:]
    c = pos[PC]
    copies = []
    for n, v in enumerate(letters):
        copies.append(pltpu.make_async_copy(v.at[rows_at(c * 512, 512)], slots.at[n], sems.at[0, n]))
        copies.append(pltpu.make_async_copy(v.at[pl.ds(LN, 16)], names.at[n], sems.at[1, n]))
    for copy in copies:
        copy.start()
    for v, (dx, dyh) in zip(letters, GATHERED):

        @pl.when(chip_of(pos, dx, dyh) == c)
        def _():
            copy = pltpu.make_async_copy(v.at[pl.ds(0, 4096)], stripe, sems.at[2, 0])
            copy.start()
            copy.wait()

    for copy in copies:
        copy.wait()


def coupled_kernel(pieces, table, pos, *refs):
    xs, (z_own, z_sib, out) = refs[:8], refs[8:]
    c, p = pos[PC], pos[PP]
    stripes = [inner_stripe(pos, dz, dyl) for dz, dyl in pieces]
    for side, (source, core) in enumerate(((z_own, p), (z_sib, 1 - p))):
        for j in range(4):
            row = Row(table, side, spot_of(pos, c), j)
            total = None
            for n in range(0, 8, 2):
                lhs, rhs = [], []
                for ref, t in zip(xs[n : n + 2], stripes[n : n + 2]):
                    lhs.append(ref[:, rows_at((row.z_name(t) - t * 8) * B)])
                    rhs.append(masked(row.z_live(t), source[rows_at(t * 512 + j * B), :]))
                term = lax.dot_general(
                    jnp.concatenate(lhs, axis=1),
                    jnp.concatenate(rhs, axis=1),
                    (((1,), (1,)), ((), ())),
                    preferred_element_type=F32,
                )
                total = term if total is None else total + term
            out[:, rows_at((core * 4 + j) * B)] = total.astype(BF)


def x_out_kernel(pieces, first, last, table, pos, *refs):
    n = len(pieces)
    blocks, rest = refs[:n], refs[n:]
    z_own, z_sib = rest[:2]
    befores = None if first else rest[2:4]
    mine, theirs, z, held, sems = rest[-5:]
    p, m = pos[PP], pos[PM]
    copies = [pltpu.make_async_copy(v, held.at[pl.ds(s * 512, 512)], sems.at[s]) for s, v in enumerate(blocks)]
    for copy in copies:
        copy.start()
    for s, (dx, dyh) in enumerate(pieces):
        t = chip_of(pos, dx, dyh)
        for side, source in enumerate((z_own, z_sib)):
            for i in range(4):
                row = Row(table, side, 0, i)
                q = row.z_name(t) - t * 8 - p * 4
                block = masked(row.z_live(t), source[i, t])
                for k in range(4):
                    at = (side * 4 + i) * B, (s * 4 + k) * B
                    z[at[0] : at[0] + B, at[1] : at[1] + B] = masked(q == k, block)
    for copy in copies:
        copy.wait()
    for side, out in enumerate((mine, theirs)):
        total = jnp.dot(z[side * 512 : side * 512 + 512, :], held[...], preferred_element_type=F32)
        if not first:
            total += befores[side][...].astype(F32)
        out[...] = total.astype(out.dtype)


def w_kernel(spots, first, last, table, pos, *refs):
    n = len(spots)
    letters, rest = refs[:n], refs[n:]
    before = None if first else rest[0]
    z_m, h_c, acc, sems = rest[-4:]
    p, m, c = pos[PP], pos[PM], pos[PC]
    copies = []
    for s, v in enumerate(letters):
        copies.append(pltpu.make_async_copy(v.at[rows_at(m * 512, 512)], z_m.at[s], sems.at[0, s]))
        copies.append(pltpu.make_async_copy(v.at[pl.ds(LH, 512)], h_c.at[s], sems.at[1, s]))
    for copy in copies:
        copy.start()
    acc[...] = jnp.zeros_like(acc) if first else before[...]
    for copy in copies:
        copy.wait()
    for s, spot in enumerate(spots):
        for j in range(4):
            row = Row(table, 0, spot, j)
            i = row.z_name(m) - m * 8
            col = row.h_name(c) - c * 8
            term = lax.dot_general(
                masked(row.z_live(m) & row.h_live(c), z_m[s, j * B : j * B + B, :]),
                h_c[s, j * B : j * B + B, :],
                (((0,), (0,)), ((), ())),
                preferred_element_type=F32,
            )
            acc[rows_at(i * B), rows_at(col * B)] += term

    if last:
        mine, theirs = rest[-6:-4]
        mine[...] = acc[rows_at(p * 512, 512), :]
        theirs[...] = acc[rows_at(512 - p * 512, 512), :].astype(BF)
    else:
        rest[-5][...] = acc[...]


def h_perp_kernel(pieces, first, last, table, pos, *refs):
    n = len(pieces)
    blocks, rest = refs[:n], refs[n:]
    own, sib = rest[:2]
    out, acc = rest[-2:]
    c, p = pos[PC], pos[PP]
    acc[...] = jnp.zeros_like(acc) if first else rest[2][...].astype(F32)
    for ref, (dz, dyl) in zip(blocks, pieces):
        spot = spot_of(pos, inner_stripe(pos, dz, dyl))
        for side, (source, core) in enumerate(((own, p), (sib, 1 - p))):
            for j in range(4):
                row = Row(table, side, spot, j)
                term = jnp.dot(
                    ref[:, rows_at((core * 4 + j) * B)],
                    masked(row.z_live(c), source[spot, j * B : j * B + B, :]),
                    preferred_element_type=F32,
                )
                acc[:, rows_at((row.z_name(c) - c * 8) * B)] += term
    out[...] = acc[...].astype(out.dtype)


def part(kernel, scalars, blocks, fixed, before, last, outs, scratch, mib, space=pltpu.VMEM):
    pieces = tuple(blocks)
    shapes = [jax.ShapeDtypeStruct((512, 1024), t) for t in outs]
    got = vmem_call(
        functools.partial(kernel, pieces, not before, last),
        scalars,
        (*blocks.values(), *fixed, *before),
        shapes,
        scratch,
        2 * 8 * len(pieces) * 512 * B * B,
        mib,
        [space] * len(pieces) + [pltpu.VMEM] * (len(fixed) + len(before)),
    )
    return list(got)


def body(h_blocks, h_cols, h_count, z_blocks, z_cols, z_count, x_perp):
    r, c = lax.axis_index("rows"), lax.axis_index("inner")
    m, p = r // 2, r % 2
    yh, ax, az, yl = m // 4, m % 4, c // 2, c % 2
    pos = jnp.stack([ax, yh, p, az, yl, m, c, r]).astype(jnp.int32)
    up_z, down_z, up_x, down_x = along_z(1), along_z(-1), along_x(1), along_x(-1)

    def at_place(v, row, column):
        return jnp.pad(v, ((row, 16 - row - v.shape[0]), (column, B - column - v.shape[1])))

    names = at_place(z_cols, 0, ZC) + at_place(h_cols, 0, HC)
    names = names + at_place(z_count[None, :], ZN, 0) + at_place(h_count[None, :], HN, 0)
    h_c = lax.dynamic_index_in_dim(h_blocks, c, 1, keepdims=False).reshape(512, B)
    z_slots = z_blocks.transpose(1, 0, 2, 3).reshape(4096, B)
    l = jnp.concatenate([z_slots, h_c, names.astype(BF)], axis=0)

    la, lb, ly = send(l, up_x), send(l, down_x), send(l, other_yh)
    xa, xb = send(x_perp, up_z), send(x_perp, down_z)
    l, la, lb, ly, z = after(l, la, lb, ly, z_blocks)
    x, xa, xb = after(x_perp, xa, xb)
    la2, lyb = send(la, up_x), send(ly, down_x)
    xy, xa2 = send(x, other_yl), send(xa, up_z)
    z_sib = send(z, other_core)
    la2, ly, lyb, z_sib = after(la2, ly, lyb, z_sib)
    xy, xa2 = after(xy, xa2)
    lya, lyb2 = send(ly, up_x), send(lyb, down_x)
    xya, xyb, xya2 = send(xy, up_z), send(xy, down_z), send(xa2, other_yl)

    tile = jax.ShapeDtypeStruct((512, 1024), BF)

    def table_of(letters):
        return jnp.stack([v[LN : LN + 6, :16] for v in letters]).astype(jnp.int32)

    def w_part(letters, names, before, last):
        shapes = [jax.ShapeDtypeStruct((512, 1024), F32), tile] if last else [jax.ShapeDtypeStruct((1024, 1024), F32)]
        n = len(letters)
        scratch = [pltpu.VMEM((n, 512, B), BF)] * 2 + [pltpu.VMEM((1024, 1024), F32), pltpu.SemaphoreType.DMA((2, n))]
        spaces = [pl.ANY] * n + [pltpu.VMEM] * len(before)
        arrays = (*[v if last else in_hbm(v) for v in letters.values()], *before)
        kernel = functools.partial(w_kernel, tuple(letters), not before, last)
        return list(vmem_call(kernel, (names, pos), arrays, shapes, scratch, 8 * n * B**3, 22, spaces))

    early = {0: l, 1: lb, 2: la2, 3: la, 4: ly, 5: lyb}
    names_early = table_of([*early.values(), l, l])[None]
    ws = w_part(early, names_early, [], False)
    lya, lyb2, xya, xyb, xya2, *ws = after(lya, lyb2, xya, xyb, xya2, *ws)

    letters = [*early.values(), lyb2, lya]
    z_stripe, slots_zc, names = vmem_call(
        pick_kernel,
        (pos,),
        [*[in_hbm(v) for v in early.values()], lyb2, lya],
        [jax.ShapeDtypeStruct((*n, B), BF) for n in ((4096,), (8, 512), (8, 16))],
        [pltpu.SemaphoreType.DMA((3, 8))],
        0,
        2,
        pl.ANY,
        pl.ANY,
    )
    table = names[:, :6, :16].astype(jnp.int32)
    table = jnp.stack([table, send(table, other_core)])
    at = (table, pos)
    z_stripe_sib = send(z_stripe, other_core)
    w_mine, w_theirs = w_part({6: lyb2, 7: lya}, table, ws, True)
    w = (w_mine + send(w_theirs, other_core).astype(F32)).astype(BF)
    x_all = {OWN: x, UP: xa, DOWN: xb, PAIR: xy, FAR: xa2, PAIR_UP: xya, PAIR_DOWN: xyb, PAIR_FAR: xya2}
    v = vmem_call(
        functools.partial(coupled_kernel, tuple(x_all)),
        at,
        (*x_all.values(), z_stripe, z_stripe_sib),
        tile,
        [],
        2 * 64 * 512 * B * B,
        18,
    )

    v, w = after(v, w)
    va, vb, vy = send(v, up_x), send(v, down_x), send(v, other_yh)
    wa, wb = send(w, up_z), send(w, down_z)
    va, vy = after(va, vy)
    vb, wa, wb, w, slots_zc = after(vb, wa, wb, w, slots_zc)
    va2, vyb = send(va, up_x), send(vy, down_x)
    wy, wa2 = send(w, other_yl), send(wa, up_z)
    slots_zc_sib = send(slots_zc, other_core)

    def x_part(blocks, before, last):
        n = len(blocks)
        scratch = [pltpu.VMEM((1024, 512 * n), BF), pltpu.VMEM((512 * n, 1024), BF), pltpu.SemaphoreType.DMA((n,))]
        outs = [F32, BF] if last else [BF, BF]
        return part(x_out_kernel, at, blocks, (z, z_sib), before, last, outs, scratch, 14 + 3 * n, pl.ANY)

    def h_part(blocks, before, last):
        scratch = [pltpu.VMEM((512, 1024), F32)]
        return part(h_perp_kernel, at, blocks, (slots_zc, slots_zc_sib), before, last, [BF], scratch, 12 + len(blocks))

    va2, vy, vyb = after(va2, vy, vyb)
    wy, wa2, slots_zc_sib = after(wy, wa2, slots_zc_sib)
    vya, vyb2 = send(vy, up_x), send(vyb, down_x)
    wya, wyb, wya2 = send(wy, up_z), send(wy, down_z), send(wa2, other_yl)
    xs = x_part({OWN: v, UP: va, DOWN: vb, PAIR: vy, FAR: va2, PAIR_DOWN: vyb}, [], False)
    hs = h_part({OWN: w, UP: wa, DOWN: wb, PAIR: wy, FAR: wa2}, [], False)
    vya, vyb2, *hs = after(vya, vyb2, *hs)
    mine, theirs = x_part({PAIR_UP: vya, PAIR_FAR: vyb2}, xs, True)
    x_tile = (mine + send(theirs, other_core).astype(F32)).astype(BF)
    (h_tile,) = h_part({PAIR_UP: wya, PAIR_DOWN: wyb, PAIR_FAR: wya2}, hs, True)
    return h_tile, x_tile


def solution(mesh):
    in_specs = (
        P("rows", None, None, None),
        P("rows", None),
        P("rows"),
        P("rows", None, None, None),
        P("rows", None),
        P("rows"),
        P("rows", "inner"),
    )
    out_specs = (P("rows", "inner"), P("rows", "inner"))
    return jax.shard_map(body, mesh=mesh, in_specs=in_specs, out_specs=out_specs, check_vma=False)
```

```python
import functools

import jax
import jax.numpy as jnp
from jax import lax
from jax.experimental import pallas as pl
from jax.experimental.pallas import tpu as pltpu
from jax.sharding import PartitionSpec as P

AXES = ("rows", "inner")
B = 128
BF = jnp.bfloat16
F32 = jnp.float32
MIB = 1024 * 1024
ZC, HC, ZN, HN = 0, 8, 4, 5
PX, PYH, PP, PZ, PYL, PM, PC, PR = range(8)


def places():
    for yh in range(2):
        for x in range(4):
            for p in range(2):
                for z in range(4):
                    for yl in range(2):
                        yield yh, x, p, z, yl


def number(yh, x, p, z, yl):
    return (((yh * 4 + x % 4) * 2 + p) * 4 + z % 4) * 2 + yl


def send(value, to):
    return lax.ppermute(value, AXES, [(number(*at), number(*to(*at))) for at in places()])


def along_x(d):
    return lambda yh, x, p, z, yl: (yh, (x + d) % 4, p, z, yl)


def along_z(d):
    return lambda yh, x, p, z, yl: (yh, x, p, (z + d) % 4, yl)


def other_yh(yh, x, p, z, yl):
    return 1 - yh, x, p, z, yl


def other_yl(yh, x, p, z, yl):
    return yh, x, p, z, 1 - yl


def other_core(yh, x, p, z, yl):
    return yh, x, 1 - p, z, yl


OWN, UP, DOWN, FAR = (0, 0), (-1, 0), (1, 0), (2, 0)
PAIR, PAIR_UP, PAIR_DOWN, PAIR_FAR = (0, 1), (-1, 1), (1, 1), (2, 1)
GATHERED = (OWN, DOWN, FAR, UP, PAIR, PAIR_DOWN, PAIR_FAR, PAIR_UP)
LZ, LH, LN, LETTER = 0, 4096, 4608, 4624


def after(*values):
    return lax.optimization_barrier(values)


def in_hbm(value):
    return pltpu.with_memory_space_constraint(value, pltpu.HBM)


def vmem_call(kernel, scalars, arrays, out_shape, scratch, flops, mib, space=pltpu.VMEM, out_space=pltpu.VMEM):
    spaces = space if isinstance(space, list) else [space] * len(arrays)
    whole_out = pl.BlockSpec(memory_space=out_space)
    many = isinstance(out_shape, (list, tuple))
    outs = list(out_shape) if many else [out_shape]
    size = sum(a.size * a.dtype.itemsize for a in list(arrays) + outs)
    return pl.pallas_call(
        kernel,
        out_shape=out_shape,
        grid_spec=pltpu.PrefetchScalarGridSpec(
            num_scalar_prefetch=len(scalars),
            grid=(),
            in_specs=[pl.BlockSpec(memory_space=v) for v in spaces],
            out_specs=[whole_out] * len(outs) if many else whole_out,
            scratch_shapes=scratch,
        ),
        compiler_params=pltpu.CompilerParams(vmem_limit_bytes=mib * MIB),
        cost_estimate=pl.CostEstimate(flops=flops, bytes_accessed=size, transcendentals=0),
    )(*scalars, *arrays)


def inner_stripe(pos, dz, dyl):
    return lax.rem(pos[PZ] + dz + 4, 4) * 2 + lax.rem(pos[PYL] + dyl, 2)


def chip_of(pos, dx, dyh):
    return lax.rem(pos[PYH] + dyh, 2) * 4 + lax.rem(pos[PX] + dx + 4, 4)


def spot_of(pos, chip):
    return lax.rem(chip // 4 + pos[PYH], 2) * 4 + lax.rem(lax.rem(chip, 4) - pos[PX] + 4, 4)


class Row:
    def __init__(self, table, side, piece, j):
        self.table, self.side, self.piece, self.j = table, side, piece, j

    def z_name(self, t):
        return self.table[self.side, self.piece, self.j, ZC + t]

    def h_name(self, s):
        return self.table[self.side, self.piece, self.j, HC + s]

    def z_live(self, t):
        return t < self.table[self.side, self.piece, ZN, self.j]

    def h_live(self, s):
        return s < self.table[self.side, self.piece, HN, self.j]


def rows_at(start, size=B):
    return pl.ds(pl.multiple_of(start, size), size)


def masked(live, block):
    return jnp.where(live, block, jnp.zeros_like(block))


def pick_kernel(pos, *refs):
    letters, (stripe, slots, names, sems) = refs[:8], refs[8:]
    c = pos[PC]
    copies = []
    for n, v in enumerate(letters):
        copies.append(pltpu.make_async_copy(v.at[rows_at(c * 512, 512)], slots.at[n], sems.at[0, n]))
        copies.append(pltpu.make_async_copy(v.at[pl.ds(LN, 16)], names.at[n], sems.at[1, n]))
    for copy in copies:
        copy.start()
    for v, (dx, dyh) in zip(letters, GATHERED):

        @pl.when(chip_of(pos, dx, dyh) == c)
        def _():
            copy = pltpu.make_async_copy(v.at[pl.ds(0, 4096)], stripe, sems.at[2, 0])
            copy.start()
            copy.wait()

    for copy in copies:
        copy.wait()


def coupled_kernel(pieces, table, pos, *refs):
    xs, (z_own, z_sib, out) = refs[:8], refs[8:]
    c, p = pos[PC], pos[PP]
    stripes = [inner_stripe(pos, dz, dyl) for dz, dyl in pieces]
    for side, (source, core) in enumerate(((z_own, p), (z_sib, 1 - p))):
        for j in range(4):
            row = Row(table, side, spot_of(pos, c), j)
            total = None
            for n in range(0, 8, 2):
                lhs, rhs = [], []
                for ref, t in zip(xs[n : n + 2], stripes[n : n + 2]):
                    lhs.append(ref[:, rows_at((row.z_name(t) - t * 8) * B)])
                    rhs.append(masked(row.z_live(t), source[rows_at(t * 512 + j * B), :]))
                term = lax.dot_general(
                    jnp.concatenate(lhs, axis=1),
                    jnp.concatenate(rhs, axis=1),
                    (((1,), (1,)), ((), ())),
                    preferred_element_type=F32,
                )
                total = term if total is None else total + term
            out[:, rows_at((core * 4 + j) * B)] = total.astype(BF)


def x_out_kernel(pieces, first, last, table, pos, *refs):
    n = len(pieces)
    blocks, rest = refs[:n], refs[n:]
    z_own, z_sib = rest[:2]
    befores = None if first else rest[2:4]
    mine, theirs, z, held, sems = rest[-5:]
    p, m = pos[PP], pos[PM]
    copies = [pltpu.make_async_copy(v, held.at[pl.ds(s * 512, 512)], sems.at[s]) for s, v in enumerate(blocks)]
    for copy in copies:
        copy.start()
    for s, (dx, dyh) in enumerate(pieces):
        t = chip_of(pos, dx, dyh)
        for side, source in enumerate((z_own, z_sib)):
            for i in range(4):
                row = Row(table, side, 0, i)
                q = row.z_name(t) - t * 8 - p * 4
                block = masked(row.z_live(t), source[i, t])
                for k in range(4):
                    at = (side * 4 + i) * B, (s * 4 + k) * B
                    z[at[0] : at[0] + B, at[1] : at[1] + B] = masked(q == k, block)
    for copy in copies:
        copy.wait()
    for side, out in enumerate((mine, theirs)):
        total = jnp.dot(z[side * 512 : side * 512 + 512, :], held[...], preferred_element_type=F32)
        if not first:
            total += befores[side][...].astype(F32)
        out[...] = total.astype(out.dtype)


def w_kernel(spots, first, last, table, pos, *refs):
    n = len(spots)
    letters, rest = refs[:n], refs[n:]
    before = None if first else rest[0]
    z_m, h_c, acc, sems = rest[-4:]
    p, m, c = pos[PP], pos[PM], pos[PC]
    copies = []
    for s, v in enumerate(letters):
        copies.append(pltpu.make_async_copy(v.at[rows_at(m * 512, 512)], z_m.at[s], sems.at[0, s]))
        copies.append(pltpu.make_async_copy(v.at[pl.ds(LH, 512)], h_c.at[s], sems.at[1, s]))
    for copy in copies:
        copy.start()
    acc[...] = jnp.zeros_like(acc) if first else before[...]
    for copy in copies:
        copy.wait()
    for s, spot in enumerate(spots):
        for j in range(4):
            row = Row(table, 0, spot, j)
            i = row.z_name(m) - m * 8
            col = row.h_name(c) - c * 8
            term = lax.dot_general(
                masked(row.z_live(m) & row.h_live(c), z_m[s, j * B : j * B + B, :]),
                h_c[s, j * B : j * B + B, :],
                (((0,), (0,)), ((), ())),
                preferred_element_type=F32,
            )
            acc[rows_at(i * B), rows_at(col * B)] += term

    if last:
        mine, theirs = rest[-6:-4]
        mine[...] = acc[rows_at(p * 512, 512), :]
        theirs[...] = acc[rows_at(512 - p * 512, 512), :].astype(BF)
    else:
        rest[-5][...] = acc[...]


def h_perp_kernel(pieces, first, last, table, pos, *refs):
    n = len(pieces)
    blocks, rest = refs[:n], refs[n:]
    own, sib = rest[:2]
    out, acc = rest[-2:]
    c, p = pos[PC], pos[PP]
    acc[...] = jnp.zeros_like(acc) if first else rest[2][...].astype(F32)
    for ref, (dz, dyl) in zip(blocks, pieces):
        spot = spot_of(pos, inner_stripe(pos, dz, dyl))
        for side, (source, core) in enumerate(((own, p), (sib, 1 - p))):
            for j in range(4):
                row = Row(table, side, spot, j)
                term = jnp.dot(
                    ref[:, rows_at((core * 4 + j) * B)],
                    masked(row.z_live(c), source[spot, j * B : j * B + B, :]),
                    preferred_element_type=F32,
                )
                acc[:, rows_at((row.z_name(c) - c * 8) * B)] += term
    out[...] = acc[...].astype(out.dtype)


def part(kernel, scalars, blocks, fixed, before, last, outs, scratch, mib, space=pltpu.VMEM):
    pieces = tuple(blocks)
    shapes = [jax.ShapeDtypeStruct((512, 1024), t) for t in outs]
    got = vmem_call(
        functools.partial(kernel, pieces, not before, last),
        scalars,
        (*blocks.values(), *fixed, *before),
        shapes,
        scratch,
        2 * 8 * len(pieces) * 512 * B * B,
        mib,
        [space] * len(pieces) + [pltpu.VMEM] * (len(fixed) + len(before)),
    )
    return list(got)


def body(h_blocks, h_cols, h_count, z_blocks, z_cols, z_count, x_perp):
    r, c = lax.axis_index("rows"), lax.axis_index("inner")
    m, p = r // 2, r % 2
    yh, ax, az, yl = m // 4, m % 4, c // 2, c % 2
    pos = jnp.stack([ax, yh, p, az, yl, m, c, r]).astype(jnp.int32)
    up_z, down_z, up_x, down_x = along_z(1), along_z(-1), along_x(1), along_x(-1)

    def at_place(v, row, column):
        return jnp.pad(v, ((row, 16 - row - v.shape[0]), (column, B - column - v.shape[1])))

    names = at_place(z_cols, 0, ZC) + at_place(h_cols, 0, HC)
    names = names + at_place(z_count[None, :], ZN, 0) + at_place(h_count[None, :], HN, 0)
    h_c = lax.dynamic_index_in_dim(h_blocks, c, 1, keepdims=False).reshape(512, B)
    z_slots = z_blocks.transpose(1, 0, 2, 3).reshape(4096, B)
    l = jnp.concatenate([z_slots, h_c, names.astype(BF)], axis=0)

    la, lb, ly = send(l, up_x), send(l, down_x), send(l, other_yh)
    xa, xb = send(x_perp, up_z), send(x_perp, down_z)
    l, la, lb, ly, z = after(l, la, lb, ly, z_blocks)
    x, xa, xb = after(x_perp, xa, xb)
    la2, lyb = send(la, up_x), send(ly, down_x)
    xy, xa2 = send(x, other_yl), send(xa, up_z)
    z_sib = send(z, other_core)
    ly, lyb = after(ly, lyb)
    la2, z_sib, xy, xa2 = after(la2, z_sib, xy, xa2)
    lya, lyb2 = send(ly, up_x), send(lyb, down_x)
    xya, xyb, xya2 = send(xy, up_z), send(xy, down_z), send(xa2, other_yl)

    tile = jax.ShapeDtypeStruct((512, 1024), BF)

    def table_of(letters):
        return jnp.stack([v[LN : LN + 6, :16] for v in letters]).astype(jnp.int32)

    def w_part(letters, names, before, last):
        shapes = [jax.ShapeDtypeStruct((512, 1024), F32), tile] if last else [jax.ShapeDtypeStruct((1024, 1024), F32)]
        n = len(letters)
        scratch = [pltpu.VMEM((n, 512, B), BF)] * 2 + [pltpu.VMEM((1024, 1024), F32), pltpu.SemaphoreType.DMA((2, n))]
        spaces = [pl.ANY] * n + [pltpu.VMEM] * len(before)
        arrays = (*[v if last else in_hbm(v) for v in letters.values()], *before)
        kernel = functools.partial(w_kernel, tuple(letters), not before, last)
        return list(vmem_call(kernel, (names, pos), arrays, shapes, scratch, 8 * n * B**3, 22, spaces))

    early = {0: l, 1: lb, 2: la2, 3: la, 4: ly, 5: lyb}
    names_early = table_of([*early.values(), l, l])[None]
    ws = w_part(early, names_early, [], False)
    lya, lyb2, xya, xyb, xya2, *ws = after(lya, lyb2, xya, xyb, xya2, *ws)

    letters = [*early.values(), lyb2, lya]
    z_stripe, slots_zc, names = vmem_call(
        pick_kernel,
        (pos,),
        [*[in_hbm(v) for v in early.values()], lyb2, lya],
        [jax.ShapeDtypeStruct((*n, B), BF) for n in ((4096,), (8, 512), (8, 16))],
        [pltpu.SemaphoreType.DMA((3, 8))],
        0,
        2,
        pl.ANY,
        pl.ANY,
    )
    table = names[:, :6, :16].astype(jnp.int32)
    table = jnp.stack([table, send(table, other_core)])
    at = (table, pos)
    z_stripe_sib = send(z_stripe, other_core)
    w_mine, w_theirs = w_part({6: lyb2, 7: lya}, table, ws, True)
    w = (w_mine + send(w_theirs, other_core).astype(F32)).astype(BF)
    x_all = {OWN: x, UP: xa, DOWN: xb, PAIR: xy, FAR: xa2, PAIR_UP: xya, PAIR_DOWN: xyb, PAIR_FAR: xya2}
    v = vmem_call(
        functools.partial(coupled_kernel, tuple(x_all)),
        at,
        (*x_all.values(), z_stripe, z_stripe_sib),
        tile,
        [],
        2 * 64 * 512 * B * B,
        18,
    )

    v, w = after(v, w)
    va, vb, vy = send(v, up_x), send(v, down_x), send(v, other_yh)
    wa, wb = send(w, up_z), send(w, down_z)
    va, vy = after(va, vy)
    vb, wa, wb, w, slots_zc = after(vb, wa, wb, w, slots_zc)
    va2, vyb = send(va, up_x), send(vy, down_x)
    wy, wa2 = send(w, other_yl), send(wa, up_z)
    slots_zc_sib = send(slots_zc, other_core)

    def x_part(blocks, before, last):
        n = len(blocks)
        scratch = [pltpu.VMEM((1024, 512 * n), BF), pltpu.VMEM((512 * n, 1024), BF), pltpu.SemaphoreType.DMA((n,))]
        outs = [F32, BF] if last else [BF, BF]
        return part(x_out_kernel, at, blocks, (z, z_sib), before, last, outs, scratch, 14 + 3 * n, pl.ANY)

    def h_part(blocks, before, last):
        scratch = [pltpu.VMEM((512, 1024), F32)]
        return part(h_perp_kernel, at, blocks, (slots_zc, slots_zc_sib), before, last, [BF], scratch, 12 + len(blocks))

    vy, vyb = after(vy, vyb)
    va2, wy, wa2, slots_zc_sib = after(va2, wy, wa2, slots_zc_sib)
    vya, vyb2 = send(vy, up_x), send(vyb, down_x)
    wya, wyb, wya2 = send(wy, up_z), send(wy, down_z), send(wa2, other_yl)
    xs = x_part({OWN: v, UP: va, DOWN: vb, PAIR: vy, FAR: va2, PAIR_DOWN: vyb}, [], False)
    hs = h_part({OWN: w, UP: wa, DOWN: wb, PAIR: wy, FAR: wa2}, [], False)
    vya, vyb2, *hs = after(vya, vyb2, *hs)
    mine, theirs = x_part({PAIR_UP: vya, PAIR_FAR: vyb2}, xs, True)
    x_tile = (mine + send(theirs, other_core).astype(F32)).astype(BF)
    (h_tile,) = h_part({PAIR_UP: wya, PAIR_DOWN: wyb, PAIR_FAR: wya2}, hs, True)
    return h_tile, x_tile


def solution(mesh):
    in_specs = (
        P("rows", None, None, None),
        P("rows", None),
        P("rows"),
        P("rows", None, None, None),
        P("rows", None),
        P("rows"),
        P("rows", "inner"),
    )
    out_specs = (P("rows", "inner"), P("rows", "inner"))
    return jax.shard_map(body, mesh=mesh, in_specs=in_specs, out_specs=out_specs, check_vma=False)
```
